256 devices in a mesh: tm: 16 (over y, x), tile: 16 (over z, core).
Axes of the slice: x: 4, y: 4, z: 8, core: 2. Of those that a mesh axis runs over, the one named last changes fastest.
Arguments:
- latents: bfloat16 [32, 32, 32, 512], P('tm', 'tile'), may hold values from -60 to 60, as said below
- norm_gain: float32 [3, 512], replicated, may hold values from 0.5 to 1.5
- norm_shift: float32 [3, 512], replicated, may hold values from -3 to 3
- conv_weight: bfloat16 [3, 27, 512, 512], P(None, None, 'tile'), may hold values from -0.0546875 to 0.0546875
- conv_bias: float32 [3, 512], P(None, 'tile'), may hold values from -3 to 3
Outputs:
- decoded: bfloat16 [32, 32, 32, 512], P('tm', 'tile')
The draws below stay inside these ranges and needn't reach their ends.
Inputs may be any that keep to these rules, and one draw needn't show every extreme that they name: Decoder input latents.
All inputs are finite; a program needn't handle non-finite values.
Results may differ from the reference program's by a relative error of at most 0.013.
Values may be sent and summed in bfloat16 or wider, within the bound.
A program may use at most 192 MiB of HBM per device.

```python
import jax
import jax.numpy as jnp
from jax import lax

C = 512
GROUPS = 32
LAYERS = 3
W = 32
NF = 32
H = 32


def draw_latents(key, part):
    key = jax.random.fold_in(key, 11)
    key_base, key_chan, key_frame = jax.random.split(key, 3)
    ramp = jnp.arange(NF, dtype=jnp.float32) / max(NF - 1, 1)
    rough = jax.random.uniform(key_frame, (NF,), jnp.float32, 0.7, 1.4)
    channel_scale = jnp.exp(jax.random.uniform(key_chan, (C,), jnp.float32, jnp.log(0.3), jnp.log(3.0)))
    base = jax.random.normal(key_base, (NF, H, W, C), jnp.float32)
    frame_scale = rough * 3.0 ** ramp
    values = base * channel_scale * frame_scale[:, None, None, None] * 0.5
    return jnp.clip(values, -60.0, 60.0).astype(jnp.bfloat16)


def block_levels(key, dims, pieces, smallest, top_value):
    level = 1.0
    for axis_at, blocks in pieces:
        draws = jax.random.uniform(jax.random.fold_in(jax.random.fold_in(key, 6), axis_at), (blocks,), jnp.float32, smallest / len(pieces), top_value / len(pieces))
        level = level * jnp.repeat(jnp.exp(draws), dims[axis_at] // blocks).reshape((-1,) + (1,) * (len(dims) - 1 - axis_at))
    return level


def scatter_about(own_key, shape, width, most, cuts=(), held_as=jnp.bfloat16):
    drawn = width * jax.random.normal(own_key, shape, jnp.float32)
    if cuts:
        drawn = drawn * block_levels(own_key, shape, cuts, -0.22, 0.18)
    return jnp.clip(drawn, -most, most).astype(held_as)


def setup_inputs(seed: int = 0) -> dict:
    key_of = jax.random.split(jax.random.key(seed), 6)
    latents = draw_latents(jax.random.fold_in(key_of[5], 71), 0)
    norm_gain = jnp.clip(1.0 + 0.1 * jax.random.normal(key_of[1], (LAYERS, C), jnp.float32), 0.5, 1.5)
    norm_shift = scatter_about(key_of[2], (LAYERS, C), 0.5, 3.0, (), jnp.float32)
    conv_weight = scatter_about(key_of[3], (LAYERS, 27, C, C), (27 * C) ** -0.5, 0.0546875, ((2, 16),))
    conv_bias = scatter_about(key_of[4], (LAYERS, C), 0.5, 3.0, ((1, 16),), jnp.float32)
    return {"latents": latents, "norm_gain": norm_gain, "norm_shift": norm_shift, "conv_weight": conv_weight, "conv_bias": conv_bias}


EPSILON = 1e-06

def normalize(latent, gain_row, shift_row):
    frames, height, breadth, channels = latent.shape
    group_width = channels // GROUPS
    values = latent.astype(jnp.float32).reshape(frames, height * breadth, GROUPS, group_width)
    first_sums = jnp.cumsum(lax.optimization_barrier(jnp.sum(values, axis=(1, 3))), axis=0)
    second_sums = jnp.cumsum(lax.optimization_barrier(jnp.sum(values * values, axis=(1, 3))), axis=0)
    counts = ((jnp.arange(frames) + 1) * (height * breadth * group_width)).astype(jnp.float32)[:, None]
    average = first_sums / counts
    inverse = lax.rsqrt(second_sums / counts - average * average + EPSILON)
    scaled = ((values - average[:, None, :, None]) * inverse[:, None, :, None]).reshape(latent.shape)
    return jax.nn.silu(scaled * gain_row + shift_row).astype(jnp.bfloat16)

def extend(active):
    return jnp.concatenate([active[:1], active[:1], active], axis=0)

def apply_kernel(cells, matrix):
    return lax.dot_general(cells, matrix, (((1,), (1,)), ((), ())), preferred_element_type=jnp.float32)

def convolve(extended, kernel):
    frames = extended.shape[0] - 2
    height, breadth = (extended.shape[1], extended.shape[2])
    spaced = jnp.pad(extended, ((0, 0), (1, 1), (1, 1), (0, 0)))
    summed = jnp.zeros((frames * height * breadth, kernel.shape[1]), jnp.float32)
    for offset in range(27):
        step_t, step_h, step_w = (offset // 9, offset // 3 % 3, offset % 3)
        window_cells = spaced[step_t:step_t + frames, step_h:step_h + height, step_w:step_w + breadth, :]
        summed = summed + apply_kernel(window_cells.reshape(-1, window_cells.shape[3]), kernel[offset])
    return summed.reshape(frames, height, breadth, kernel.shape[1])

def reference(latents, norm_gain, norm_shift, conv_weight, conv_bias):
    hidden = (convolve(extend(normalize(latents, norm_gain[0], norm_shift[0])), conv_weight[0]) + conv_bias[0]).astype(jnp.bfloat16)
    branch = convolve(extend(normalize(hidden, norm_gain[1], norm_shift[1])), conv_weight[1]) + conv_bias[1]
    block = (latents.astype(jnp.float32) + branch).astype(jnp.bfloat16)
    return (convolve(extend(normalize(block, norm_gain[2], norm_shift[2])), conv_weight[2]) + conv_bias[2]).astype(jnp.bfloat16)
```

```python
import jax
import jax.numpy as jnp
from jax import lax
from jax.experimental import pallas as pl
from jax.experimental.pallas import tpu as pltpu
from jax.sharding import PartitionSpec as P

MESH = pl.DeviceIdType.MESH
BF, F32 = jnp.bfloat16, jnp.float32
EPSILON = 1e-06
LAYERS = 3
MAIN = 10 * 256
TOP = MAIN
BOT = MAIN + 512
LANES = MAIN + 1024
HALF = LANES // 2
PER_FRAME = 32 * 32 * 16


def lane_of(shape):
    return lax.broadcasted_iota(jnp.int32, shape, len(shape) - 1)


def roll(x, shift):
    size = x.shape[-1]
    shift = shift % size
    return x if shift == 0 else pltpu.roll(x, shift, axis=x.ndim - 1)


def silu(v):
    return v / (1.0 + jnp.exp(-v))


def kernel(
    lat_ref, gain_ref, shift_ref, w_hbm, bias_ref, out_ref,
    w_ref, local_t, slots_in, raw, top_out, bot_out, top_in, bot_in, top_prev, bot_prev,
    stat_out, stat_in, y_ref, slots_out, final_t, par_ref,
    w_sem, a2a_send, a2a_recv, fin_send, fin_recv, stat_send, stat_recv,
    halo_send, halo_recv, ring_send, ring_recv, sib_send, sib_recv,
):
    tm = lax.axis_index("tm")
    tile = lax.axis_index("tile")
    x, y = lax.rem(tm, 4), lax.div(tm, 4)
    z, core = lax.div(tile, 2), lax.rem(tile, 2)
    chans = pl.multiple_of(tile * 32, 32)
    sibling = z * 2 + (1 - core)
    right = lax.rem(z + 1, 8) * 2 + core
    left = lax.rem(z + 7, 8) * 2 + core

    def remote(src, dst, send, recv, to_tm, to_tile):
        return pltpu.make_async_remote_copy(
            src_ref=src, dst_ref=dst, send_sem=send, recv_sem=recv,
            device_id=(to_tm, to_tile), device_id_type=MESH,
        )

    load_w = pltpu.make_async_copy(w_hbm, w_ref, w_sem)
    load_w.start()

    mine = lat_ref[...].reshape(128, 512).astype(F32)
    local_t[...] = mine.T.astype(BF)
    my_slot = x * 4 + lax.rem(tile, 4)

    def in_copy(t):
        return remote(
            local_t.at[pl.ds(pl.multiple_of(t * 32, 32), 32)], slots_in.at[my_slot],
            a2a_send, a2a_recv, y * 4 + lax.div(tile, 4), t,
        )

    own_x = lax.div(tile, 4) == x

    def send_in(t, carry):
        to_self = jnp.logical_and(t == tile, own_x)

        @pl.when(to_self)
        def _():
            pltpu.make_async_copy(
                local_t.at[pl.ds(pl.multiple_of(t * 32, 32), 32)], slots_in.at[my_slot], a2a_recv
            ).start()

        @pl.when(jnp.logical_not(to_self))
        def _():
            in_copy(t).start()

        return carry

    lax.fori_loop(0, 16, send_in, 0)

    par_ref[...] = jnp.zeros_like(par_ref)
    par_ref[0:3, :] = gain_ref[...]
    par_ref[3:6, :] = shift_ref[...]
    picked = pltpu.roll(par_ref[...], lax.rem(512 - tile * 32, 512), axis=1)[:, :128]
    par_ref[...] = jnp.zeros_like(par_ref)
    par_ref[0:3, 0:32] = bias_ref[...]
    columns = jnp.concatenate([picked, par_ref[:, 0:128], jnp.zeros((112, 128), F32)], axis=0)
    columns = columns.T[0:32]
    par_ref[0:8, 0:128] = columns[0:8]
    par_ref[0:8, 128:256] = columns[8:16]
    par_ref[0:8, 256:384] = columns[16:24]
    par_ref[0:8, 384:512] = columns[24:32]

    def column(index):
        all_columns = jnp.concatenate([par_ref[0:8, 128 * i:128 * i + 128] for i in range(4)], axis=0)
        chosen = jnp.where(lane_of((32, 128)) == index, all_columns, 0.0)
        return jnp.sum(chosen, axis=1, keepdims=True)

    pltpu.make_async_copy(slots_in, slots_in, a2a_recv).wait()
    lane128 = lane_of((32, 128))
    for part in range(4):
        for block in range(2):
            one = slots_in[part * 4 + 2 * block].astype(F32)
            two = slots_in[part * 4 + 2 * block + 1].astype(F32)
            for inner in range(2):
                if inner == 0:
                    frame = jnp.where(lane128 < 64, one, roll(two, 64))
                else:
                    frame = jnp.where(lane128 < 64, roll(one, 64), two)
                at = 256 * (2 + 2 * part + inner) + 128 * block
                raw[0, :, at:at + 128] = frame.astype(BF)

    lane256 = lane_of((32, 256))
    col256, row256 = lax.rem(lane256, 32), lax.div(lane256, 32)

    def ring_copy(layer, way, step):
        back = (step - 1) if way == 0 else (1 - step)
        owner = lax.rem(z - back + 8, 8) * 2 + core
        rows = pl.ds(pl.multiple_of(owner * 32, 32), 32)
        lanes = slice(0, LANES)
        if step == 4:
            lanes = slice(0, HALF) if way == 0 else slice(HALF, LANES)
        piece = y_ref.at[layer, rows, lanes]
        return remote(
            piece, piece, ring_send.at[layer, way * 4 + step - 1], ring_recv.at[layer, way * 4 + step - 1],
            tm, right if way == 0 else left,
        )

    def sib_copy(layer, back, lanes, index):
        owner = lax.rem(z - back + 8, 8) * 2 + core
        rows = pl.ds(pl.multiple_of(owner * 32, 32), 32)
        piece = y_ref.at[layer, rows, lanes]
        return remote(piece, piece, sib_send.at[layer, index], sib_recv.at[layer, index], tm, sibling)

    whole = slice(0, LANES)
    sib_parts = [
        (0, whole, 0), (1, whole, 1), (-1, whole, 2), (2, whole, 3), (-2, whole, 4),
        (3, whole, 5), (-3, whole, 6), (4, slice(0, HALF), 7), (-4, slice(HALF, LANES), 8),
    ]

    def halo_copies(layer):
        to_left, to_right = lax.rem(x + 3, 4), lax.rem(x + 1, 4)
        later = lax.rem(y + 1, 4)
        plan = [
            (top_out, bot_in, y * 4 + to_left), (bot_out, top_in, y * 4 + to_right),
            (top_out, bot_prev, later * 4 + to_left), (bot_out, top_prev, later * 4 + to_right),
        ]
        copies = [
            remote(src.at[layer], dst.at[layer], halo_send.at[layer, i], halo_recv.at[layer, i], to, tile)
            for i, (src, dst, to) in enumerate(plan)
        ]
        copies.append(remote(
            raw.at[layer, :, 256 * 8:256 * 10], raw.at[layer, :, 0:512],
            halo_send.at[layer, 4], halo_recv.at[layer, 4], later * 4 + x, tile,
        ))
        return copies

    def stat_copy(layer, k):
        other = lax.rem(tm + k, 16)
        return remote(
            stat_out.at[layer], stat_in.at[layer, 15 - k], stat_send.at[layer], stat_recv.at[layer], other, tile
        )

    def layer_step(layer, carry):
        halos = halo_copies(layer)
        halos[4].start()
        sums = jnp.zeros((32, 128), F32)
        tops = [jnp.zeros((32, 128), F32)] * 2
        bots = [jnp.zeros((32, 128), F32)] * 2
        for f in range(8):
            values = raw[layer, :, 256 * (f + 2):256 * (f + 3)].astype(F32)
            first = jnp.sum(values, axis=1, keepdims=True)
            second = jnp.sum(values * values, axis=1, keepdims=True)
            sums = jnp.where(lane128 == f, first, sums)
            sums = jnp.where(lane128 == 8 + f, second, sums)
            slot = f // 2
            here = lax.div(lane128, 32) == slot
            tops[f % 2] = jnp.where(here, roll(values[:, :128], 32 * slot), tops[f % 2])
            bots[f % 2] = jnp.where(here, roll(values[:, 128:], 32 * slot - 96), bots[f % 2])
        for i in range(2):
            top_out[layer, :, 128 * i:128 * i + 128] = tops[i].astype(BF)
            bot_out[layer, :, 128 * i:128 * i + 128] = bots[i].astype(BF)
        low = jnp.sum(sums[0:16], axis=0, keepdims=True)
        high = jnp.sum(sums[16:32], axis=0, keepdims=True)
        sub8 = lax.broadcasted_iota(jnp.int32, (8, 128), 0)
        stat_out[layer] = jnp.where(sub8 == 0, low, jnp.where(sub8 == 1, high, 0.0))

        def send_stat(k, c):
            stat_copy(layer, k).start()
            return c

        lax.fori_loop(1, 16, send_stat, 0)
        for copy in halos[:4]:
            copy.start()

        pltpu.make_async_copy(stat_in.at[layer], stat_in.at[layer], stat_recv.at[layer]).wait()
        mask_lane = lax.broadcasted_iota(jnp.int32, (128, 128), 0)
        mask_col = lax.broadcasted_iota(jnp.int32, (128, 128), 1)
        wanted = jnp.maximum(8 * y - 2 + lax.rem(mask_col, 16), 0)
        fits = (mask_lane < 16) & (mask_col < 32) & (lax.div(mask_lane, 8) == lax.div(mask_col, 16))
        sources = [jnp.zeros((8, 128), F32)] * 4
        for s in range(16):
            block = stat_out[layer] if s == 15 else stat_in[layer, s]
            from_y = lax.div(lax.rem(tm + 16 - (15 - s), 16), 4)
            for q in range(4):
                sources[q] = sources[q] + jnp.where(from_y == q, block, 0.0)
        cumulative = jnp.zeros((8, 128), F32)
        for q in range(4):
            mask = jnp.where(fits & (8 * q + lax.rem(mask_lane, 8) <= wanted), 1.0, 0.0)
            cumulative = cumulative + lax.dot_general(
                sources[q], mask, (((1,), (0,)), ((), ())),
                precision=lax.Precision.HIGHEST, preferred_element_type=F32,
            )
        lane8 = lane_of((8, 128))
        count = ((jnp.maximum(8 * y - 2 + lax.rem(lane8, 16), 0) + 1) * PER_FRAME).astype(F32)
        average = cumulative / count
        spread = roll(average, -16)
        inverse = lax.rsqrt(spread - average * average + EPSILON)
        low_half = lax.broadcasted_iota(jnp.int32, (32, 128), 0) < 16
        average = jnp.where(low_half, average[0:1], average[1:2])
        inverse = jnp.where(low_half, inverse[0:1], inverse[1:2])
        gain, shift = column(layer), column(3 + layer)

        def normal(values, mean_at, inverse_at):
            return silu(((values - mean_at) * inverse_at) * gain + shift)

        for copy in halos:
            copy.wait_recv()
        mine = pl.ds(chans, 32)
        opening = y == 0
        for j in range(10):
            values = raw[layer, :, 256 * j:256 * j + 256].astype(F32)
            if j < 2:
                values = jnp.where(opening, raw[layer, :, 512:768].astype(F32), values)
            done = normal(values, average[:, j:j + 1], inverse[:, j:j + 1])
            y_ref[layer, mine, 256 * j:256 * j + 256] = done.astype(BF)
        slot128 = lax.div(lane128, 32)
        for base, now, before, outside in (
            (TOP, top_in, top_prev, x == 0), (BOT, bot_in, bot_prev, x == 3),
        ):
            even = now[layer, :, 0:128].astype(F32)
            for b in range(4):
                own = now[layer, :, 128 * (b % 2):128 * (b % 2) + 128].astype(F32)
                values = own
                if b < 2:
                    earlier = roll(before[layer, :, 128 * b:128 * b + 128].astype(F32), 32)
                    earlier = jnp.where(opening, even, earlier)
                    values = jnp.where(slot128 == 0, earlier, roll(own, 32))
                mean_at, inverse_at = average[:, b:b + 1], inverse[:, b:b + 1]
                for s in range(1, 4):
                    j = b + 2 * s
                    mean_at = jnp.where(slot128 == s, average[:, j:j + 1], mean_at)
                    inverse_at = jnp.where(slot128 == s, inverse[:, j:j + 1], inverse_at)
                done = jnp.where(outside, 0.0, normal(values, mean_at, inverse_at))
                y_ref[layer, mine, base + 128 * b:base + 128 * b + 128] = done.astype(BF)

        ring_copy(layer, 0, 1).start()
        ring_copy(layer, 1, 1).start()
        sib_copy(layer, *sib_parts[0]).start()
        for step in range(1, 5):
            for way in (0, 1):
                ring_copy(layer, way, step).wait_recv()
                if step < 4:
                    ring_copy(layer, way, step + 1).start()
                sib_copy(layer, *sib_parts[2 * step - 1 + way]).start()
        for part in sib_parts:
            sib_copy(layer, *part).wait_recv()

        @pl.when(layer == 0)
        def _():
            load_w.wait()

        def product(first_offset, count, lanes_at):
            total = None
            for dt in range(3):
                matrix = w_ref[layer, pl.ds(9 * dt + first_offset, count)].reshape(32 * count, 512)
                cells = y_ref[layer, :, lanes_at(dt)]
                term = lax.dot_general(
                    matrix, cells, (((1,), (0,)), ((), ())), preferred_element_type=F32
                )
                total = term if total is None else total + term
            return total

        def across(total):
            before = jnp.where(col256 >= 1, roll(total[0:32], 1), 0.0)
            after = jnp.where(col256 <= 30, roll(total[64:96], -1), 0.0)
            return before + total[32:64] + after

        upper = across(product(0, 3, lambda dt: slice(TOP + 128 * dt, TOP + 128 * dt + 256)))
        lower = across(product(6, 3, lambda dt: slice(BOT + 128 * dt, BOT + 128 * dt + 256)))
        bias = column(8 + layer)
        keep = jnp.where(layer == 1, 1.0, 0.0)
        for f in range(8):
            total = product(0, 9, lambda dt: slice(256 * (f + dt), 256 * (f + dt) + 256))
            above = roll(across(total[0:96]), 32)
            below = roll(across(total[192:288]), -32)
            slot = f // 2
            edge = 128 * (f % 2)
            from_upper = roll(upper[:, edge:edge + 128], -32 * slot)
            from_lower = roll(lower[:, edge:edge + 128], 96 - 32 * slot)
            zero = jnp.zeros((32, 128), F32)
            above = jnp.where(row256 == 0, jnp.concatenate([from_upper, zero], axis=1), above)
            below = jnp.where(row256 == 7, jnp.concatenate([zero, from_lower], axis=1), below)
            result = above + across(total[96:192]) + below + bias
            result = result + keep * raw[0, :, 256 * (f + 2):256 * (f + 3)].astype(F32)
            raw[layer + 1, :, 256 * (f + 2):256 * (f + 3)] = result.astype(BF)
        return carry

    lax.fori_loop(0, LAYERS, layer_step, 0)

    for part in range(4):
        for block in range(2):
            at = 256 * (2 + 2 * part) + 128 * block
            one = raw[LAYERS, :, at:at + 128].astype(F32)
            two = raw[LAYERS, :, at + 256:at + 384].astype(F32)
            slots_out[part * 4 + 2 * block] = jnp.where(lane128 < 64, one, roll(two, 64)).astype(BF)
            slots_out[part * 4 + 2 * block + 1] = jnp.where(lane128 < 64, roll(one, 64), two).astype(BF)

    def send_out(slot, c):
        to_tm = y * 4 + lax.div(slot, 4)
        to_tile = x * 4 + lax.rem(slot, 4)
        to_self = jnp.logical_and(to_tm == tm, to_tile == tile)
        rows = final_t.at[pl.ds(chans, 32)]

        @pl.when(to_self)
        def _():
            pltpu.make_async_copy(slots_out.at[slot], rows, fin_recv).start()

        @pl.when(jnp.logical_not(to_self))
        def _():
            remote(slots_out.at[slot], rows, fin_send, fin_recv, to_tm, to_tile).start()

        return c

    lax.fori_loop(0, 16, send_out, 0)
    pltpu.make_async_copy(final_t, final_t, fin_recv).wait()
    out_ref[...] = final_t[...].astype(F32).T.astype(BF).reshape(2, 2, 32, 512)


    def sent(ref, sem):
        @pl.when(own_x)
        def _():
            pltpu.make_async_copy(ref.at[0:15], ref.at[0:15], sem).wait()

        @pl.when(jnp.logical_not(own_x))
        def _():
            pltpu.make_async_copy(ref, ref, sem).wait()

    sent(slots_in, a2a_send)
    sent(slots_out, fin_send)

    def drain(layer, c):
        for copy in halo_copies(layer):
            copy.wait_send()
        pltpu.make_async_copy(stat_in.at[layer], stat_in.at[layer], stat_send.at[layer]).wait()
        for step in range(1, 5):
            for way in (0, 1):
                ring_copy(layer, way, step).wait_send()
        for part in sib_parts:
            sib_copy(layer, *part).wait_send()
        return c

    lax.fori_loop(0, LAYERS, drain, 0)


def on_device(latents, norm_gain, norm_shift, conv_weight, conv_bias):
    vmem = pl.BlockSpec(memory_space=pltpu.VMEM)
    dma = pltpu.SemaphoreType.DMA
    return pl.pallas_call(
        kernel,
        out_shape=jax.ShapeDtypeStruct((2, 2, 32, 512), BF),
        in_specs=[vmem, vmem, vmem, pl.BlockSpec(memory_space=pl.ANY), vmem],
        out_specs=vmem,
        scratch_shapes=[
            pltpu.VMEM((3, 27, 32, 512), BF),
            pltpu.VMEM((512, 128), BF),
            pltpu.VMEM((16, 32, 128), BF),
            pltpu.VMEM((4, 32, MAIN), BF),
            pltpu.VMEM((3, 32, 256), BF),
            pltpu.VMEM((3, 32, 256), BF),
            pltpu.VMEM((3, 32, 256), BF),
            pltpu.VMEM((3, 32, 256), BF),
            pltpu.VMEM((3, 32, 256), BF),
            pltpu.VMEM((3, 32, 256), BF),
            pltpu.VMEM((3, 8, 128), F32),
            pltpu.VMEM((3, 15, 8, 128), F32),
            pltpu.VMEM((3, 512, LANES), BF),
            pltpu.VMEM((16, 32, 128), BF),
            pltpu.VMEM((512, 128), BF),
            pltpu.VMEM((8, 512), F32),
            dma, dma, dma, dma, dma, dma((3,)), dma((3,)),
            dma((3, 5)), dma((3, 5)), dma((3, 8)), dma((3, 8)), dma((3, 9)), dma((3, 9)),
        ],
        compiler_params=pltpu.CompilerParams(
            has_side_effects=True, vmem_limit_bytes=50 * 1024 * 1024
        ),
        cost_estimate=pl.CostEstimate(flops=8 * 10**9, bytes_accessed=3 * 10**6, transcendentals=10**6),
    )(latents, norm_gain, norm_shift, conv_weight, conv_bias)


def solution(mesh):
    placed = (P("tm", "tile", None, None), P(), P(), P(None, None, "tile", None), P(None, "tile"))
    return jax.shard_map(
        on_device,
        mesh=mesh,
        in_specs=placed,
        out_specs=P("tm", "tile", None, None),
        check_vma=False,
    )
```

```python
import jax
import jax.numpy as jnp
from jax import lax
from jax.experimental import pallas as pl
from jax.experimental.pallas import tpu as pltpu
from jax.sharding import PartitionSpec as P

MESH = pl.DeviceIdType.MESH
BF, F32 = jnp.bfloat16, jnp.float32
EPSILON = 1e-06
LAYERS = 3
MAIN = 10 * 256
TOP = MAIN
BOT = MAIN + 256
PREV = MAIN + 512
LANES = MAIN + 640
CHUNKS = ((0, 1664), (1664, LANES))
PARTS = len(CHUNKS)
PER_FRAME = 32 * 32 * 16


def lane_of(shape):
    return lax.broadcasted_iota(jnp.int32, shape, len(shape) - 1)


def roll(x, shift):
    size = x.shape[-1]
    shift = shift % size
    return x if shift == 0 else pltpu.roll(x, shift, axis=x.ndim - 1)


def silu(v):
    return v / (1.0 + jnp.exp(-v))


def kernel(
    lat_hbm, gain_hbm, shift_hbm, w_hbm, bias_hbm, out_ref,
    lat_ref, gain_ref, shift_ref, bias_ref,
    w_ref, local_t, slots_in, raw, top_out, bot_out, top_in, bot_in, top_prev, bot_prev,
    stat_out, stat_in, y_ref, slots_out, final_t, par_ref,
    in_sem, w_sem, a2a_send, a2a_recv, fin_send, fin_recv, stat_send, stat_recv,
    halo_send, halo_recv, ring_send, ring_recv, sib_send, sib_recv,
):
    tm = lax.axis_index("tm")
    tile = lax.axis_index("tile")
    x, y = lax.rem(tm, 4), lax.div(tm, 4)
    z, core = lax.div(tile, 2), lax.rem(tile, 2)
    chans = pl.multiple_of(tile * 32, 32)
    sibling = z * 2 + (1 - core)
    right = lax.rem(z + 1, 8) * 2 + core
    left = lax.rem(z + 7, 8) * 2 + core

    def remote(src, dst, send, recv, to_tm, to_tile):
        return pltpu.make_async_remote_copy(
            src_ref=src, dst_ref=dst, send_sem=send, recv_sem=recv,
            device_id=(to_tm, to_tile), device_id_type=MESH,
        )

    load_w = pltpu.make_async_copy(w_hbm, w_ref, w_sem)
    loads = [
        pltpu.make_async_copy(src, dst, in_sem.at[i])
        for i, (src, dst) in enumerate((
            (lat_hbm, lat_ref), (gain_hbm, gain_ref), (shift_hbm, shift_ref), (bias_hbm, bias_ref),
        ))
    ]
    for load in loads:
        load.start()
    load_w.start()

    barrier = pltpu.get_barrier_semaphore()
    own_x = lax.div(tile, 4) == x

    def greet(to_tm, to_tile):
        pl.semaphore_signal(barrier, inc=1, device_id=(to_tm, to_tile), device_id_type=MESH)

    def greet_tm(k, c):
        greet(lax.rem(tm + k, 16), tile)
        return c

    def greet_a2a(k, c):
        to_tm = y * 4 + lax.div(tile, 4)

        @pl.when(jnp.logical_not(jnp.logical_and(to_tm == tm, k == tile)))
        def _():
            greet(to_tm, k)

        from_tm, from_tile = y * 4 + lax.div(k, 4), x * 4 + lax.rem(k, 4)

        @pl.when(jnp.logical_not(jnp.logical_and(from_tm == tm, from_tile == tile)))
        def _():
            greet(from_tm, from_tile)

        return c

    lax.fori_loop(0, 16, greet_a2a, 0)
    lax.fori_loop(1, 16, greet_tm, 0)
    greet(tm, sibling)
    greet(tm, left)
    greet(tm, right)

    loads[0].wait()
    mine = lat_ref[...].reshape(128, 512).astype(F32)
    local_t[...] = mine.T.astype(BF)
    my_slot = x * 4 + lax.rem(tile, 4)

    def in_copy(t):
        return remote(
            local_t.at[pl.ds(pl.multiple_of(t * 32, 32), 32)], slots_in.at[my_slot],
            a2a_send, a2a_recv, y * 4 + lax.div(tile, 4), t,
        )

    def send_in(t, carry):
        to_self = jnp.logical_and(t == tile, own_x)

        @pl.when(to_self)
        def _():
            pltpu.make_async_copy(
                local_t.at[pl.ds(pl.multiple_of(t * 32, 32), 32)], slots_in.at[my_slot], a2a_recv
            ).start()

        @pl.when(jnp.logical_not(to_self))
        def _():
            in_copy(t).start()

        return carry

    pl.semaphore_wait(barrier, jnp.where(own_x, 48, 50))
    lax.fori_loop(0, 16, send_in, 0)

    for load in loads[1:]:
        load.wait()
    par_ref[...] = jnp.zeros_like(par_ref)
    par_ref[0:3, :] = gain_ref[...]
    par_ref[3:6, :] = shift_ref[...]
    picked = pltpu.roll(par_ref[...], lax.rem(512 - tile * 32, 512), axis=1)[:, :128]
    par_ref[...] = jnp.zeros_like(par_ref)
    par_ref[0:3, 0:32] = bias_ref[...]
    columns = jnp.concatenate([picked, par_ref[:, 0:128], jnp.zeros((112, 128), F32)], axis=0)
    columns = columns.T[0:32]
    par_ref[0:8, 0:128] = columns[0:8]
    par_ref[0:8, 128:256] = columns[8:16]
    par_ref[0:8, 256:384] = columns[16:24]
    par_ref[0:8, 384:512] = columns[24:32]

    def column(index):
        all_columns = jnp.concatenate([par_ref[0:8, 128 * i:128 * i + 128] for i in range(4)], axis=0)
        chosen = jnp.where(lane_of((32, 128)) == index, all_columns, 0.0)
        return jnp.sum(chosen, axis=1, keepdims=True)

    pltpu.make_async_copy(slots_in, slots_in, a2a_recv).wait()
    lane128 = lane_of((32, 128))
    for part in range(4):
        for block in range(2):
            one = slots_in[part * 4 + 2 * block].astype(F32)
            two = slots_in[part * 4 + 2 * block + 1].astype(F32)
            for inner in range(2):
                if inner == 0:
                    frame = jnp.where(lane128 < 64, one, roll(two, 64))
                else:
                    frame = jnp.where(lane128 < 64, roll(one, 64), two)
                at = 256 * (2 + 2 * part + inner) + 128 * block
                raw[0, :, at:at + 128] = frame.astype(BF)

    lane256 = lane_of((32, 256))
    col256, row256 = lax.rem(lane256, 32), lax.div(lane256, 32)

    def ring_copy(layer, way, step, part):
        back = (step - 1) if way == 0 else (1 - step)
        owner = lax.rem(z - back + 8, 8) * 2 + core
        rows = pl.ds(pl.multiple_of(owner * 32, 32), 32)
        piece = y_ref.at[layer, rows, slice(*CHUNKS[part])]
        at = (way * 4 + step - 1) * PARTS + part
        return remote(
            piece, piece, ring_send.at[layer, at], ring_recv.at[layer, at], tm, right if way == 0 else left
        )

    ring_order = [
        (way, step, part)
        for step in range(1, 5) for part in range(PARTS) for way in (0, 1)
        if step < 4 or (part < PARTS // 2) == (way == 0)
    ]

    def sib_copy(layer, back, lanes, at):
        owner = lax.rem(z - back + 8, 8) * 2 + core
        rows = pl.ds(pl.multiple_of(owner * 32, 32), 32)
        piece = y_ref.at[layer, rows, slice(*lanes)]
        return remote(piece, piece, sib_send.at[layer, at], sib_recv.at[layer, at], tm, sibling)

    sib_order = [(0, (0, LANES), 0)] + [
        (step if way == 0 else -step, CHUNKS[part], 1 + i) for i, (way, step, part) in enumerate(ring_order)
    ]

    def halo_copies(layer):
        to_left, to_right = lax.rem(x + 3, 4), lax.rem(x + 1, 4)
        later = lax.rem(y + 1, 4)
        plan = [
            (top_out, bot_in, y * 4 + to_left), (bot_out, top_in, y * 4 + to_right),
            (top_out, bot_prev, later * 4 + to_left), (bot_out, top_prev, later * 4 + to_right),
        ]
        copies = [
            remote(src.at[layer], dst.at[layer], halo_send.at[layer, i], halo_recv.at[layer, i], to, tile)
            for i, (src, dst, to) in enumerate(plan)
        ]
        copies.append(remote(
            raw.at[layer, :, 256 * 8:256 * 10], raw.at[layer, :, 0:512],
            halo_send.at[layer, 4], halo_recv.at[layer, 4], later * 4 + x, tile,
        ))
        return copies

    def stat_copy(layer, k):
        other = lax.rem(tm + k, 16)
        return remote(
            stat_out.at[layer], stat_in.at[layer, 15 - k], stat_send.at[layer], stat_recv.at[layer], other, tile
        )

    def layer_step(layer, carry):
        halos = halo_copies(layer)
        halos[4].start()
        sums = jnp.zeros((32, 128), F32)
        tops = [jnp.zeros((32, 128), F32)] * 2
        bots = [jnp.zeros((32, 128), F32)] * 2
        for f in range(8):
            values = raw[layer, :, 256 * (f + 2):256 * (f + 3)].astype(F32)
            first = jnp.sum(values, axis=1, keepdims=True)
            second = jnp.sum(values * values, axis=1, keepdims=True)
            sums = jnp.where(lane128 == f, first, sums)
            sums = jnp.where(lane128 == 8 + f, second, sums)
            slot = f // 2
            here = lax.div(lane128, 32) == slot
            tops[f % 2] = jnp.where(here, roll(values[:, :128], 32 * slot), tops[f % 2])
            bots[f % 2] = jnp.where(here, roll(values[:, 128:], 32 * slot - 96), bots[f % 2])
        for i in range(2):
            top_out[layer, :, 128 * i:128 * i + 128] = tops[i].astype(BF)
            bot_out[layer, :, 128 * i:128 * i + 128] = bots[i].astype(BF)
        low = jnp.sum(sums[0:16], axis=0, keepdims=True)
        high = jnp.sum(sums[16:32], axis=0, keepdims=True)
        sub8 = lax.broadcasted_iota(jnp.int32, (8, 128), 0)
        stat_out[layer] = jnp.where(sub8 == 0, low, jnp.where(sub8 == 1, high, 0.0))

        def send_stat(k, c):
            stat_copy(layer, k).start()
            return c

        lax.fori_loop(1, 16, send_stat, 0)
        for copy in halos[:4]:
            copy.start()

        pltpu.make_async_copy(stat_in.at[layer], stat_in.at[layer], stat_recv.at[layer]).wait()
        mask_lane = lax.broadcasted_iota(jnp.int32, (128, 128), 0)
        mask_col = lax.broadcasted_iota(jnp.int32, (128, 128), 1)
        wanted = jnp.maximum(8 * y - 2 + lax.rem(mask_col, 16), 0)
        fits = (mask_lane < 16) & (mask_col < 32) & (lax.div(mask_lane, 8) == lax.div(mask_col, 16))
        sources = [jnp.zeros((8, 128), F32)] * 4
        for s in range(16):
            block = stat_out[layer] if s == 15 else stat_in[layer, s]
            from_y = lax.div(lax.rem(tm + 16 - (15 - s), 16), 4)
            for q in range(4):
                sources[q] = sources[q] + jnp.where(from_y == q, block, 0.0)
        cumulative = jnp.zeros((8, 128), F32)
        for q in range(4):
            mask = jnp.where(fits & (8 * q + lax.rem(mask_lane, 8) <= wanted), 1.0, 0.0)
            cumulative = cumulative + lax.dot_general(
                sources[q], mask, (((1,), (0,)), ((), ())),
                precision=lax.Precision.HIGHEST, preferred_element_type=F32,
            )
        lane8 = lane_of((8, 128))
        count = ((jnp.maximum(8 * y - 2 + lax.rem(lane8, 16), 0) + 1) * PER_FRAME).astype(F32)
        average = cumulative / count
        spread = roll(average, -16)
        inverse = lax.rsqrt(spread - average * average + EPSILON)
        low_half = lax.broadcasted_iota(jnp.int32, (32, 128), 0) < 16
        average = jnp.where(low_half, average[0:1], average[1:2])
        inverse = jnp.where(low_half, inverse[0:1], inverse[1:2])
        gain, shift = column(layer), column(3 + layer)

        def normal(values, mean_at, inverse_at):
            return silu(((values - mean_at) * inverse_at) * gain + shift)

        for copy in halos:
            copy.wait_recv()
        mine = pl.ds(chans, 32)
        opening = y == 0
        for j in range(10):
            values = raw[layer, :, 256 * j:256 * j + 256].astype(F32)
            if j < 2:
                values = jnp.where(opening, raw[layer, :, 512:768].astype(F32), values)
            done = normal(values, average[:, j:j + 1], inverse[:, j:j + 1])
            y_ref[layer, mine, 256 * j:256 * j + 256] = done.astype(BF)
        slot128 = lax.div(lane128, 32)
        for base, now, outside in ((TOP, top_in, x == 0), (BOT, bot_in, x == 3)):
            for b in range(2):
                values = now[layer, :, 128 * b:128 * b + 128].astype(F32)
                mean_at, inverse_at = average[:, b + 2:b + 3], inverse[:, b + 2:b + 3]
                for s in range(1, 4):
                    j = b + 2 + 2 * s
                    mean_at = jnp.where(slot128 == s, average[:, j:j + 1], mean_at)
                    inverse_at = jnp.where(slot128 == s, inverse[:, j:j + 1], inverse_at)
                done = jnp.where(outside, 0.0, normal(values, mean_at, inverse_at))
                y_ref[layer, mine, base + 128 * b:base + 128 * b + 128] = done.astype(BF)
        values = jnp.zeros((32, 128), F32)
        for i, (now, before) in enumerate(((top_in, top_prev), (bot_in, bot_prev))):
            first = now[layer, :, 0:128].astype(F32)
            for b in range(2):
                last = before[layer, :, 128 * b:128 * b + 128].astype(F32)
                slot = 2 * i + b
                moved = jnp.where(opening, roll(first, 32 * slot), roll(last, 32 * slot - 96))
                values = jnp.where(slot128 == slot, moved, values)
        odd = lax.rem(slot128, 2) == 1
        mean_at = jnp.where(odd, average[:, 1:2], average[:, 0:1])
        inverse_at = jnp.where(odd, inverse[:, 1:2], inverse[:, 0:1])
        done = normal(values, mean_at, inverse_at)
        done = jnp.where((slot128 < 2) & (x == 0) | (slot128 >= 2) & (x == 3), 0.0, done)
        y_ref[layer, mine, PREV:PREV + 128] = done.astype(BF)

        for part in range(PARTS):
            for way in (0, 1):
                ring_copy(layer, way, 1, part).start()
        sib_copy(layer, *sib_order[0]).start()
        for i, (way, step, part) in enumerate(ring_order):
            ring_copy(layer, way, step, part).wait_recv()
            if (way, step + 1, part) in ring_order:
                ring_copy(layer, way, step + 1, part).start()
            sib_copy(layer, *sib_order[1 + i]).start()
        for entry in sib_order:
            sib_copy(layer, *entry).wait_recv()

        @pl.when(layer == 0)
        def _():
            load_w.wait()

        def product(first_offset, count, lanes_at):
            total = None
            for dt in range(3):
                matrix = w_ref[layer, pl.ds(9 * dt + first_offset, count)].reshape(32 * count, 512)
                cells = y_ref[layer, :, lanes_at(dt)]
                term = lax.dot_general(
                    matrix, cells, (((1,), (0,)), ((), ())), preferred_element_type=F32
                )
                total = term if total is None else total + term
            return total

        def across(total):
            before = jnp.where(col256 >= 1, roll(total[0:32], 1), 0.0)
            after = jnp.where(col256 <= 30, roll(total[64:96], -1), 0.0)
            return before + total[32:64] + after

        def edge_rows(base, first_offset, slot):
            early, late, now = [
                lax.dot_general(
                    w_ref[layer, pl.ds(9 * dt + first_offset, 3)].reshape(96, 512),
                    y_ref[layer, :, base:base + 256],
                    (((1,), (0,)), ((), ())), preferred_element_type=F32,
                )
                for dt in range(3)
            ]
            before, middle = [
                lax.dot_general(
                    w_ref[layer, pl.ds(9 * dt + first_offset, 3)].reshape(96, 512),
                    y_ref[layer, :, PREV:PREV + 128],
                    (((1,), (0,)), ((), ())), preferred_element_type=F32,
                )
                for dt in range(2)
            ]
            slots = lax.div(lane_of((96, 128)), 32)
            even = roll(early[:, :128] + late[:, 128:], 32)
            odd = roll(early[:, 128:], 32)
            even = jnp.where(slots == 0, roll(before, -32 * slot) + roll(middle, -32 * slot - 32), even)
            odd = jnp.where(slots == 0, roll(before, -32 * slot - 32), odd)
            even = even + now[:, :128]
            odd = odd + late[:, :128] + now[:, 128:]
            return across(jnp.concatenate([even, odd], axis=1))

        upper = edge_rows(TOP, 0, 0)
        lower = edge_rows(BOT, 6, 2)
        bias = column(8 + layer)
        keep = jnp.where(layer == 1, 1.0, 0.0)
        for f in range(8):
            total = product(0, 9, lambda dt: slice(256 * (f + dt), 256 * (f + dt) + 256))
            above = roll(across(total[0:96]), 32)
            below = roll(across(total[192:288]), -32)
            slot = f // 2
            edge = 128 * (f % 2)
            from_upper = roll(upper[:, edge:edge + 128], -32 * slot)
            from_lower = roll(lower[:, edge:edge + 128], 96 - 32 * slot)
            zero = jnp.zeros((32, 128), F32)
            above = jnp.where(row256 == 0, jnp.concatenate([from_upper, zero], axis=1), above)
            below = jnp.where(row256 == 7, jnp.concatenate([zero, from_lower], axis=1), below)
            result = above + across(total[96:192]) + below + bias
            result = result + keep * raw[0, :, 256 * (f + 2):256 * (f + 3)].astype(F32)
            raw[layer + 1, :, 256 * (f + 2):256 * (f + 3)] = result.astype(BF)
        return carry

    lax.fori_loop(0, LAYERS, layer_step, 0)

    for part in range(4):
        for block in range(2):
            at = 256 * (2 + 2 * part) + 128 * block
            one = raw[LAYERS, :, at:at + 128].astype(F32)
            two = raw[LAYERS, :, at + 256:at + 384].astype(F32)
            slots_out[part * 4 + 2 * block] = jnp.where(lane128 < 64, one, roll(two, 64)).astype(BF)
            slots_out[part * 4 + 2 * block + 1] = jnp.where(lane128 < 64, roll(one, 64), two).astype(BF)

    def send_out(slot, c):
        to_tm = y * 4 + lax.div(slot, 4)
        to_tile = x * 4 + lax.rem(slot, 4)
        to_self = jnp.logical_and(to_tm == tm, to_tile == tile)
        rows = final_t.at[pl.ds(chans, 32)]

        @pl.when(to_self)
        def _():
            pltpu.make_async_copy(slots_out.at[slot], rows, fin_recv).start()

        @pl.when(jnp.logical_not(to_self))
        def _():
            remote(slots_out.at[slot], rows, fin_send, fin_recv, to_tm, to_tile).start()

        return c

    lax.fori_loop(0, 16, send_out, 0)
    pltpu.make_async_copy(final_t, final_t, fin_recv).wait()
    out_ref[...] = final_t[...].astype(F32).T.astype(BF).reshape(2, 2, 32, 512)


    def sent(ref, sem):
        @pl.when(own_x)
        def _():
            pltpu.make_async_copy(ref.at[0:15], ref.at[0:15], sem).wait()

        @pl.when(jnp.logical_not(own_x))
        def _():
            pltpu.make_async_copy(ref, ref, sem).wait()

    sent(slots_in, a2a_send)
    sent(slots_out, fin_send)

    def drain(layer, c):
        for copy in halo_copies(layer):
            copy.wait_send()
        pltpu.make_async_copy(stat_in.at[layer], stat_in.at[layer], stat_send.at[layer]).wait()
        for entry in ring_order:
            ring_copy(layer, *entry).wait_send()
        for entry in sib_order:
            sib_copy(layer, *entry).wait_send()
        return c

    lax.fori_loop(0, LAYERS, drain, 0)


def on_device(latents, norm_gain, norm_shift, conv_weight, conv_bias):
    vmem = pl.BlockSpec(memory_space=pltpu.VMEM)
    dma = pltpu.SemaphoreType.DMA
    return pl.pallas_call(
        kernel,
        out_shape=jax.ShapeDtypeStruct((2, 2, 32, 512), BF),
        in_specs=[pl.BlockSpec(memory_space=pltpu.HBM)] * 5,
        out_specs=vmem,
        scratch_shapes=[
            pltpu.VMEM((2, 2, 32, 512), BF),
            pltpu.VMEM((3, 512), F32),
            pltpu.VMEM((3, 512), F32),
            pltpu.VMEM((3, 32), F32),
            pltpu.VMEM((3, 27, 32, 512), BF),
            pltpu.VMEM((512, 128), BF),
            pltpu.VMEM((16, 32, 128), BF),
            pltpu.VMEM((4, 32, MAIN), BF),
            pltpu.VMEM((3, 32, 256), BF),
            pltpu.VMEM((3, 32, 256), BF),
            pltpu.VMEM((3, 32, 256), BF),
            pltpu.VMEM((3, 32, 256), BF),
            pltpu.VMEM((3, 32, 256), BF),
            pltpu.VMEM((3, 32, 256), BF),
            pltpu.VMEM((3, 8, 128), F32),
            pltpu.VMEM((3, 15, 8, 128), F32),
            pltpu.VMEM((3, 512, LANES), BF),
            pltpu.VMEM((16, 32, 128), BF),
            pltpu.VMEM((512, 128), BF),
            pltpu.VMEM((8, 512), F32),
            dma((4,)), dma, dma, dma, dma, dma, dma((3,)), dma((3,)), dma((3, 5)), dma((3, 5)),
            dma((3, 8 * PARTS)), dma((3, 8 * PARTS)), dma((3, 8 * PARTS)), dma((3, 8 * PARTS)),
        ],
        compiler_params=pltpu.CompilerParams(
            collective_id=0, has_side_effects=True, vmem_limit_bytes=50 * 1024 * 1024
        ),
        cost_estimate=pl.CostEstimate(flops=8 * 10**9, bytes_accessed=3 * 10**6, transcendentals=10**6),
    )(latents, norm_gain, norm_shift, conv_weight, conv_bias)


def solution(mesh):
    placed = (P("tm", "tile", None, None), P(), P(), P(None, None, "tile", None), P(None, "tile"))
    return jax.shard_map(
        on_device,
        mesh=mesh,
        in_specs=placed,
        out_specs=P("tm", "tile", None, None),
        check_vma=False,
    )
```

```python
import jax
import jax.numpy as jnp
from jax import lax
from jax.experimental import pallas as pl
from jax.experimental.pallas import tpu as pltpu
from jax.sharding import PartitionSpec as P

MESH = pl.DeviceIdType.MESH
BF, F32 = jnp.bfloat16, jnp.float32
EPSILON = 1e-06
LAYERS = 3
MAIN = 10 * 256
TOP = MAIN
BOT = MAIN + 256
PREV = MAIN + 512
LANES = MAIN + 640
SENT = LANES - 512
PARTS = ((0, 1024), (1024, 2048), (2048, SENT))
PER_FRAME = 32 * 32 * 16


def lane_of(shape):
    return lax.broadcasted_iota(jnp.int32, shape, len(shape) - 1)


def roll(x, shift):
    size = x.shape[-1]
    shift = shift % size
    return x if shift == 0 else pltpu.roll(x, shift, axis=x.ndim - 1)


def silu(v):
    half = 0.5 * v
    return half + half * jnp.tanh(half)


def kernel(
    lat_hbm, gain_hbm, shift_hbm, w_hbm, bias_hbm, out_ref,
    lat_ref, gain_ref, shift_ref, bias_ref,
    w_ref, local_t, slots_in, raw, before, own, top_out, bot_out, top_in, bot_in, top_prev, bot_prev,
    stat_out, stat_in, mask_ref, coef, y_ref, slots_out, final_t, par_ref, column_ref, bias_col,
    in_sem, w_sem, a2a_send, a2a_recv, fin_send, fin_recv, stat_send, stat_recv, coef_send, coef_recv,
    halo_send, halo_recv, later_send, later_recv, ring_send, ring_recv, sib_send, sib_recv,
):
    tm = lax.axis_index("tm")
    tile = lax.axis_index("tile")
    x, y = lax.rem(tm, 4), lax.div(tm, 4)
    z, core = lax.div(tile, 2), lax.rem(tile, 2)
    chans = pl.multiple_of(tile * 32, 32)
    sibling = z * 2 + (1 - core)
    right = lax.rem(z + 1, 8) * 2 + core
    left = lax.rem(z + 7, 8) * 2 + core

    def remote(src, dst, send, recv, to_tm, to_tile):
        return pltpu.make_async_remote_copy(
            src_ref=src, dst_ref=dst, send_sem=send, recv_sem=recv,
            device_id=(to_tm, to_tile), device_id_type=MESH,
        )

    load_w = pltpu.make_async_copy(w_hbm, w_ref, w_sem)
    loads = [
        pltpu.make_async_copy(src, dst, in_sem.at[i])
        for i, (src, dst) in enumerate((
            (lat_hbm, lat_ref), (gain_hbm, gain_ref), (shift_hbm, shift_ref), (bias_hbm, bias_ref),
        ))
    ]
    for load in loads:
        load.start()
    load_w.start()

    barrier = pltpu.get_barrier_semaphore()
    own_x = lax.div(tile, 4) == x

    def greet(to_tm, to_tile):
        pl.semaphore_signal(barrier, inc=1, device_id=(to_tm, to_tile), device_id_type=MESH)

    def greet_tm(k, c):
        greet(lax.rem(tm + k, 16), tile)
        return c

    def greet_a2a(k, c):
        to_tm = y * 4 + lax.div(tile, 4)

        @pl.when(jnp.logical_not(jnp.logical_and(to_tm == tm, k == tile)))
        def _():
            greet(to_tm, k)

        from_tm, from_tile = y * 4 + lax.div(k, 4), x * 4 + lax.rem(k, 4)

        @pl.when(jnp.logical_not(jnp.logical_and(from_tm == tm, from_tile == tile)))
        def _():
            greet(from_tm, from_tile)

        return c

    lax.fori_loop(0, 16, greet_a2a, 0)
    lax.fori_loop(1, 16, greet_tm, 0)
    greet(tm, sibling)
    for k in range(1, 8):
        greet(tm, lax.rem(z + k, 8) * 2 + core)

    loads[0].wait()
    mine = lat_ref[...].reshape(128, 512).astype(F32)
    local_t[...] = mine.T.astype(BF)
    my_slot = x * 4 + lax.rem(tile, 4)

    def in_copy(t):
        return remote(
            local_t.at[pl.ds(pl.multiple_of(t * 32, 32), 32)], slots_in.at[my_slot],
            a2a_send, a2a_recv, y * 4 + lax.div(tile, 4), t,
        )

    def send_in(t, carry):
        to_self = jnp.logical_and(t == tile, own_x)

        @pl.when(to_self)
        def _():
            pltpu.make_async_copy(
                local_t.at[pl.ds(pl.multiple_of(t * 32, 32), 32)], slots_in.at[my_slot], a2a_recv
            ).start()

        @pl.when(jnp.logical_not(to_self))
        def _():
            in_copy(t).start()

        return carry

    pl.semaphore_wait(barrier, jnp.where(own_x, 53, 55))
    lax.fori_loop(0, 16, send_in, 0)

    for load in loads[1:]:
        load.wait()
    par_ref[...] = jnp.zeros_like(par_ref)
    par_ref[0:3, :] = gain_ref[...]
    par_ref[3:6, :] = shift_ref[...]
    columns = jnp.concatenate([par_ref[...], jnp.zeros((120, 512), F32)], axis=0)
    column_ref[...] = columns.T.reshape(8, 2, 32, 128)
    par_ref[...] = jnp.zeros_like(par_ref)
    par_ref[0:3, 0:32] = bias_ref[...]
    columns = jnp.concatenate([par_ref[:, 0:128], jnp.zeros((120, 128), F32)], axis=0)
    bias_col[...] = columns.T[0:32]

    def column(table, index):
        return jnp.sum(jnp.where(lane_of((32, 128)) == index, table, 0.0), axis=1, keepdims=True)

    mask_lane = lax.broadcasted_iota(jnp.int32, (128, 128), 0)
    mask_col = lax.broadcasted_iota(jnp.int32, (128, 128), 1)
    wanted = jnp.maximum(8 * y - 2 + lax.rem(mask_col, 16), 0)
    fits = (mask_lane < 16) & (mask_col < 32) & (lax.div(mask_lane, 8) == lax.div(mask_col, 16))
    for q in range(4):
        mask_ref[q] = jnp.where(fits & (8 * q + lax.rem(mask_lane, 8) <= wanted), 1.0, 0.0)

    pltpu.make_async_copy(slots_in, slots_in, a2a_recv).wait()
    lane128 = lane_of((32, 128))
    for part in range(4):
        for block in range(2):
            one = slots_in[part * 4 + 2 * block].astype(F32)
            two = slots_in[part * 4 + 2 * block + 1].astype(F32)
            for inner in range(2):
                if inner == 0:
                    frame = jnp.where(lane128 < 64, one, roll(two, 64))
                else:
                    frame = jnp.where(lane128 < 64, roll(one, 64), two)
                at = 256 * (2 * part + inner) + 128 * block
                frame = frame.astype(BF)
                raw[0, z, :, at:at + 128] = frame
                own[:, at:at + 128] = frame

    lane256 = lane_of((32, 256))
    col256, row256 = lax.rem(lane256, 32), lax.div(lane256, 32)

    def ring_copy(layer, way, step, part):
        owner = lax.rem(z + 8 + ((1 - step) if way == 0 else (step - 1)), 8)
        piece = raw.at[layer, owner, :, slice(*PARTS[part])]
        at = (way * 4 + step - 1) * 3 + part
        return remote(
            piece, piece, ring_send.at[layer, at], ring_recv.at[layer, at], tm, right if way == 0 else left
        )

    ring_order = [
        (way, step, part)
        for step in range(1, 5) for part in range(3) for way in (0, 1)
        if step < 4 or (part == 1) == (way == 1)
    ]

    def later_copy(layer, owner):
        return remote(
            raw.at[layer, owner, :, 1536:2048], before.at[layer, owner],
            later_send.at[layer, owner], later_recv.at[layer, owner], lax.rem(y + 1, 4) * 4 + x, tile,
        )

    def sib_copy(layer, owner, kind):
        piece = y_ref.at[layer, owner, core, :, slice(*((512, LANES), (0, 512))[kind])]
        return remote(
            piece, piece, sib_send.at[layer, kind, owner], sib_recv.at[layer, kind, owner], tm, sibling
        )

    def coef_copy(layer, k):
        to = lax.rem(z + k, 8) * 2 + core
        return remote(
            coef.at[layer, z], coef.at[layer, z], coef_send.at[layer], coef_recv.at[layer], tm, to
        )

    def halo_copies(layer):
        to_left, to_right = lax.rem(x + 3, 4), lax.rem(x + 1, 4)
        later = lax.rem(y + 1, 4)
        plan = [
            (top_out, bot_in, y * 4 + to_left), (bot_out, top_in, y * 4 + to_right),
            (top_out, bot_prev, later * 4 + to_left), (bot_out, top_prev, later * 4 + to_right),
        ]
        copies = [
            remote(src.at[layer], dst.at[layer], halo_send.at[layer, i], halo_recv.at[layer, i], to, tile)
            for i, (src, dst, to) in enumerate(plan)
        ]
        return copies

    def stat_copy(layer, k):
        other = lax.rem(tm + k, 16)
        return remote(
            stat_out.at[layer], stat_in.at[layer, 15 - k], stat_send.at[layer], stat_recv.at[layer], other, tile
        )

    slot128 = lax.div(lane128, 32)
    low_half = lax.broadcasted_iota(jnp.int32, (32, 128), 0) < 16
    opening = y == 0

    def coefficients(layer, owner):
        table = coef[layer, owner]
        table = jnp.where(low_half, table[0:1], table[1:2])
        columns = column_ref[owner, core]
        scaled = table * column(columns, layer)
        return table, scaled, column(columns, 3 + layer)

    def normal_own(layer, owner):
        average, scaled, shift = coefficients(layer, owner)
        for f in range(8):
            j = f + 2
            values = raw[layer, owner, :, 256 * f:256 * f + 256].astype(F32)
            values = (values - average[:, j:j + 1]) * scaled[:, 16 + j:17 + j] + shift
            y_ref[layer, owner, core, :, 256 * j:256 * j + 256] = silu(values).astype(BF)
        for b in range(5):
            if b == 4:
                frames = (0, 1, 0, 1)
                outside = (slot128 < 2) & (x == 0) | (slot128 >= 2) & (x == 3)
            else:
                frames = [b % 2 + 2 + 2 * s for s in range(4)]
                outside = (x == 0) if b < 2 else (x == 3)
            at = 2048 + 128 * b
            values = raw[layer, owner, :, at:at + 128].astype(F32)
            average_at, scaled_at = average[:, frames[0]:frames[0] + 1], scaled[:, 16 + frames[0]:17 + frames[0]]
            for s in range(1, 4):
                j = frames[s]
                average_at = jnp.where(slot128 == s, average[:, j:j + 1], average_at)
                scaled_at = jnp.where(slot128 == s, scaled[:, 16 + j:17 + j], scaled_at)
            values = jnp.where(outside, 0.0, silu((values - average_at) * scaled_at + shift))
            y_ref[layer, owner, core, :, MAIN + 128 * b:MAIN + 128 * b + 128] = values.astype(BF)
        sib_copy(layer, owner, 0).start()

    def normal_before(layer, owner):
        average, scaled, shift = coefficients(layer, owner)
        for j in range(2):
            values = before[layer, owner, :, 256 * j:256 * j + 256].astype(F32)
            values = jnp.where(opening, raw[layer, owner, :, 0:256].astype(F32), values)
            values = (values - average[:, j:j + 1]) * scaled[:, 16 + j:17 + j] + shift
            y_ref[layer, owner, core, :, 256 * j:256 * j + 256] = silu(values).astype(BF)
        sib_copy(layer, owner, 1).start()

    def layer_step(layer, carry):
        for part in range(2):
            for way in (0, 1):
                ring_copy(layer, way, 1, part).start()
        later_copy(layer, z).start()
        halos = halo_copies(layer)
        sums = jnp.zeros((32, 128), F32)
        tops = [jnp.zeros((32, 128), F32)] * 2
        bots = [jnp.zeros((32, 128), F32)] * 2
        for f in range(8):
            values = own[:, 256 * f:256 * f + 256].astype(F32)
            first = jnp.sum(values, axis=1, keepdims=True)
            second = jnp.sum(values * values, axis=1, keepdims=True)
            sums = jnp.where(lane128 == f, first, sums)
            sums = jnp.where(lane128 == 8 + f, second, sums)
            slot = f // 2
            here = lax.div(lane128, 32) == slot
            tops[f % 2] = jnp.where(here, roll(values[:, :128], 32 * slot), tops[f % 2])
            bots[f % 2] = jnp.where(here, roll(values[:, 128:], 32 * slot - 96), bots[f % 2])
        for i in range(2):
            top_out[layer, :, 128 * i:128 * i + 128] = tops[i].astype(BF)
            bot_out[layer, :, 128 * i:128 * i + 128] = bots[i].astype(BF)
        low = jnp.sum(sums[0:16], axis=0, keepdims=True)
        high = jnp.sum(sums[16:32], axis=0, keepdims=True)
        sub8 = lax.broadcasted_iota(jnp.int32, (8, 128), 0)
        stat_out[layer] = jnp.where(sub8 == 0, low, jnp.where(sub8 == 1, high, 0.0))

        for copy in halos:
            copy.start()

        def send_stat(k, c):
            stat_copy(layer, k).start()
            return c

        lax.fori_loop(1, 16, send_stat, 0)

        for copy in halos:
            copy.wait_recv()
        raw[layer, z, :, 2048:2304] = top_in[layer]
        raw[layer, z, :, 2304:2560] = bot_in[layer]
        values = jnp.zeros((32, 128), F32)
        for i, (now, earlier) in enumerate(((top_in, top_prev), (bot_in, bot_prev))):
            first = now[layer, :, 0:128].astype(F32)
            for b in range(2):
                last = earlier[layer, :, 128 * b:128 * b + 128].astype(F32)
                slot = 2 * i + b
                moved = jnp.where(opening, roll(first, 32 * slot), roll(last, 32 * slot - 96))
                values = jnp.where(slot128 == slot, moved, values)
        raw[layer, z, :, 2560:2688] = values.astype(BF)
        for way in (0, 1):
            ring_copy(layer, way, 1, 2).start()

        def pass_on(at_step):
            for way, step, part in ring_order:
                if step == at_step:
                    ring_copy(layer, way, step, part).wait_recv()
                    if (way, step + 1, part) in ring_order:
                        ring_copy(layer, way, step + 1, part).start()
                    if part == 1:
                        owner = lax.rem(z + 8 + (-step if way == 0 else step), 8)
                        later_copy(layer, owner).start()

        pass_on(1)

        pltpu.make_async_copy(stat_in.at[layer], stat_in.at[layer], stat_recv.at[layer]).wait()
        sources = [jnp.zeros((8, 128), F32)] * 4
        for s in range(16):
            block = stat_out[layer] if s == 15 else stat_in[layer, s]
            from_y = lax.div(lax.rem(tm + 16 - (15 - s), 16), 4)
            for q in range(4):
                sources[q] = sources[q] + jnp.where(from_y == q, block, 0.0)
        cumulative = jnp.zeros((8, 128), F32)
        for q in range(4):
            cumulative = cumulative + lax.dot_general(
                sources[q], mask_ref[q], (((1,), (0,)), ((), ())),
                precision=lax.Precision.HIGHEST, preferred_element_type=F32,
            )
        lane8 = lane_of((8, 128))
        count = ((jnp.maximum(8 * y - 2 + lax.rem(lane8, 16), 0) + 1) * PER_FRAME).astype(F32)
        average = cumulative / count
        spread = roll(average, -16)
        inverse = lax.rsqrt(spread - average * average + EPSILON)
        coef[layer, z] = jnp.where(lane8 < 16, average, roll(inverse, 16))
        for k in range(1, 8):
            coef_copy(layer, k).start()
        normal_own(layer, z)
        pass_on(2)
        pltpu.make_async_copy(coef.at[layer, 0:7], coef.at[layer, 0:7], coef_recv.at[layer]).wait()

        def both(work):
            def one(way, c):
                work(way)
                return c

            lax.fori_loop(0, 2, one, 0)

        def at_distance(step):
            return lambda way: lax.rem(z + 8 + (1 - 2 * way) * step, 8)

        def own_rows(step):
            owner = at_distance(step)
            both(lambda way: normal_own(layer, owner(way)))

        def rows_before(step):
            owner = at_distance(step)

            def work(way):
                later_copy(layer, owner(way)).wait_recv()
                normal_before(layer, owner(way))

            both(work)

        own_rows(1)
        pass_on(3)
        own_rows(2)
        later_copy(layer, z).wait_recv()
        normal_before(layer, z)
        rows_before(1)
        pass_on(4)
        own_rows(3)
        far = lax.rem(z + 4, 8)
        normal_own(layer, far)
        rows_before(2)
        rows_before(3)
        later_copy(layer, far).wait_recv()
        normal_before(layer, far)

        def from_sibling(owner, c):
            for kind in range(2):
                piece = y_ref.at[layer, owner, 1 - core, :, slice(*((512, LANES), (0, 512))[kind])]
                pltpu.make_async_copy(piece, piece, sib_recv.at[layer, kind, owner]).wait()
            return c

        lax.fori_loop(0, 8, from_sibling, 0)

        @pl.when(layer == 0)
        def _():
            load_w.wait()

        def product(first_offset, count, lanes_at):
            total = None
            for dt in range(3):
                matrix = w_ref[layer, pl.ds(9 * dt + first_offset, count)].reshape(32 * count, 512)
                cells = y_ref[layer, :, :, :, lanes_at(dt)].reshape(512, 256)
                term = lax.dot_general(
                    matrix, cells, (((1,), (0,)), ((), ())), preferred_element_type=F32
                )
                total = term if total is None else total + term
            return total

        def across(total):
            before = jnp.where(col256 >= 1, roll(total[0:32], 1), 0.0)
            after = jnp.where(col256 <= 30, roll(total[64:96], -1), 0.0)
            return before + total[32:64] + after

        def edge_rows(base, first_offset, slot):
            early, late, now = [
                lax.dot_general(
                    w_ref[layer, pl.ds(9 * dt + first_offset, 3)].reshape(96, 512),
                    y_ref[layer, :, :, :, base:base + 256].reshape(512, 256),
                    (((1,), (0,)), ((), ())), preferred_element_type=F32,
                )
                for dt in range(3)
            ]
            before, middle = [
                lax.dot_general(
                    w_ref[layer, pl.ds(9 * dt + first_offset, 3)].reshape(96, 512),
                    y_ref[layer, :, :, :, PREV:PREV + 128].reshape(512, 128),
                    (((1,), (0,)), ((), ())), preferred_element_type=F32,
                )
                for dt in range(2)
            ]
            slots = lax.div(lane_of((96, 128)), 32)
            even = roll(early[:, :128] + late[:, 128:], 32)
            odd = roll(early[:, 128:], 32)
            even = jnp.where(slots == 0, roll(before, -32 * slot) + roll(middle, -32 * slot - 32), even)
            odd = jnp.where(slots == 0, roll(before, -32 * slot - 32), odd)
            even = even + now[:, :128]
            odd = odd + late[:, :128] + now[:, 128:]
            return across(jnp.concatenate([even, odd], axis=1))

        upper = edge_rows(TOP, 0, 0)
        lower = edge_rows(BOT, 6, 2)
        bias = column(bias_col[...], layer)
        keep = jnp.where(layer == 1, 1.0, 0.0)
        for f in range(8):
            total = product(0, 9, lambda dt: slice(256 * (f + dt), 256 * (f + dt) + 256))
            above = roll(across(total[0:96]), 32)
            below = roll(across(total[192:288]), -32)
            slot = f // 2
            edge = 128 * (f % 2)
            from_upper = roll(upper[:, edge:edge + 128], -32 * slot)
            from_lower = roll(lower[:, edge:edge + 128], 96 - 32 * slot)
            zero = jnp.zeros((32, 128), F32)
            above = jnp.where(row256 == 0, jnp.concatenate([from_upper, zero], axis=1), above)
            below = jnp.where(row256 == 7, jnp.concatenate([zero, from_lower], axis=1), below)
            result = above + across(total[96:192]) + below + bias
            here = slice(256 * f, 256 * f + 256)
            result = result + keep * raw[0, z, :, here].astype(F32)
            result = result.astype(BF)
            own[:, here] = result

            @pl.when(layer + 1 < LAYERS)
            def _():
                raw[layer + 1, z, :, here] = result

        return carry

    lax.fori_loop(0, LAYERS, layer_step, 0)

    for part in range(4):
        for block in range(2):
            at = 512 * part + 128 * block
            one = own[:, at:at + 128].astype(F32)
            two = own[:, at + 256:at + 384].astype(F32)
            slots_out[part * 4 + 2 * block] = jnp.where(lane128 < 64, one, roll(two, 64)).astype(BF)
            slots_out[part * 4 + 2 * block + 1] = jnp.where(lane128 < 64, roll(one, 64), two).astype(BF)

    def send_out(slot, c):
        to_tm = y * 4 + lax.div(slot, 4)
        to_tile = x * 4 + lax.rem(slot, 4)
        to_self = jnp.logical_and(to_tm == tm, to_tile == tile)
        rows = final_t.at[pl.ds(chans, 32)]

        @pl.when(to_self)
        def _():
            pltpu.make_async_copy(slots_out.at[slot], rows, fin_recv).start()

        @pl.when(jnp.logical_not(to_self))
        def _():
            remote(slots_out.at[slot], rows, fin_send, fin_recv, to_tm, to_tile).start()

        return c

    lax.fori_loop(0, 16, send_out, 0)
    pltpu.make_async_copy(final_t, final_t, fin_recv).wait()
    out_ref[...] = final_t[...].astype(F32).T.astype(BF).reshape(2, 2, 32, 512)


    def sent(ref, sem):
        @pl.when(own_x)
        def _():
            pltpu.make_async_copy(ref.at[0:15], ref.at[0:15], sem).wait()

        @pl.when(jnp.logical_not(own_x))
        def _():
            pltpu.make_async_copy(ref, ref, sem).wait()

    sent(slots_in, a2a_send)
    sent(slots_out, fin_send)

    def drain(layer, c):
        for copy in halo_copies(layer):
            copy.wait_send()
        pltpu.make_async_copy(stat_in.at[layer], stat_in.at[layer], stat_send.at[layer]).wait()
        pltpu.make_async_copy(coef.at[layer, 0:7], coef.at[layer, 0:7], coef_send.at[layer]).wait()
        for entry in ring_order:
            ring_copy(layer, *entry).wait_send()

        def drain_owner(owner, carry):
            later_copy(layer, owner).wait_send()
            for kind in range(2):
                sib_copy(layer, owner, kind).wait_send()
            return carry

        lax.fori_loop(0, 8, drain_owner, 0)
        return c

    lax.fori_loop(0, LAYERS, drain, 0)


def on_device(latents, norm_gain, norm_shift, conv_weight, conv_bias):
    vmem = pl.BlockSpec(memory_space=pltpu.VMEM)
    dma = pltpu.SemaphoreType.DMA
    return pl.pallas_call(
        kernel,
        out_shape=jax.ShapeDtypeStruct((2, 2, 32, 512), BF),
        in_specs=[pl.BlockSpec(memory_space=pltpu.HBM)] * 5,
        out_specs=vmem,
        scratch_shapes=[
            pltpu.VMEM((2, 2, 32, 512), BF),
            pltpu.VMEM((3, 512), F32),
            pltpu.VMEM((3, 512), F32),
            pltpu.VMEM((3, 32), F32),
            pltpu.VMEM((3, 27, 32, 512), BF),
            pltpu.VMEM((512, 128), BF),
            pltpu.VMEM((16, 32, 128), BF),
            pltpu.VMEM((3, 8, 32, SENT), BF),
            pltpu.VMEM((3, 8, 32, 512), BF),
            pltpu.VMEM((32, 2048), BF),
            pltpu.VMEM((3, 32, 256), BF),
            pltpu.VMEM((3, 32, 256), BF),
            pltpu.VMEM((3, 32, 256), BF),
            pltpu.VMEM((3, 32, 256), BF),
            pltpu.VMEM((3, 32, 256), BF),
            pltpu.VMEM((3, 32, 256), BF),
            pltpu.VMEM((3, 8, 128), F32),
            pltpu.VMEM((3, 15, 8, 128), F32),
            pltpu.VMEM((4, 128, 128), F32),
            pltpu.VMEM((3, 8, 8, 128), F32),
            pltpu.VMEM((3, 8, 2, 32, LANES), BF),
            pltpu.VMEM((16, 32, 128), BF),
            pltpu.VMEM((512, 128), BF),
            pltpu.VMEM((8, 512), F32),
            pltpu.VMEM((8, 2, 32, 128), F32),
            pltpu.VMEM((32, 128), F32),
            dma((4,)), dma, dma, dma, dma, dma, dma((3,)), dma((3,)), dma((3,)), dma((3,)),
            dma((3, 4)), dma((3, 4)), dma((3, 8)), dma((3, 8)),
            dma((3, 24)), dma((3, 24)), dma((3, 2, 8)), dma((3, 2, 8)),
        ],
        compiler_params=pltpu.CompilerParams(
            collective_id=0, has_side_effects=True, vmem_limit_bytes=64 * 1024 * 1024
        ),
        cost_estimate=pl.CostEstimate(flops=8 * 10**9, bytes_accessed=3 * 10**6, transcendentals=10**6),
    )(latents, norm_gain, norm_shift, conv_weight, conv_bias)


def solution(mesh):
    placed = (P("tm", "tile", None, None), P(), P(), P(None, None, "tile", None), P(None, "tile"))
    return jax.shard_map(
        on_device,
        mesh=mesh,
        in_specs=placed,
        out_specs=P("tm", "tile", None, None),
        check_vma=False,
    )
```

```python
import jax
import jax.numpy as jnp
from jax import lax
from jax.experimental import pallas as pl
from jax.experimental.pallas import tpu as pltpu
from jax.sharding import PartitionSpec as P

MESH = pl.DeviceIdType.MESH
BF, F32 = jnp.bfloat16, jnp.float32
EPSILON = 1e-06
LAYERS = 3
MAIN = 10 * 256
TOP = MAIN
BOT = MAIN + 256
PREV = MAIN + 512
LANES = MAIN + 640
SENT = LANES - 512
PARTS = ((0, 1024), (1024, 2048), (2048, SENT))
PER_FRAME = 32 * 32 * 16


def lane_of(shape):
    return lax.broadcasted_iota(jnp.int32, shape, len(shape) - 1)


def roll(x, shift):
    size = x.shape[-1]
    shift = shift % size
    return x if shift == 0 else pltpu.roll(x, shift, axis=x.ndim - 1)


def silu(v):
    half = 0.5 * v
    return half + half * jnp.tanh(half)


def kernel(
    lat_hbm, gain_hbm, shift_hbm, w_hbm, bias_hbm, out_ref,
    lat_ref, gain_ref, shift_ref, bias_ref,
    w_ref, local_t, slots_in, raw, before, top_out, bot_out, top_in, bot_in, top_prev, bot_prev,
    stat_out, stat_in, mask_ref, coef, y_ref, slots_out, mid, final_t, par_ref, column_ref, bias_col, table_ref, wk_ref, part_ref,
    in_sem, w_sem, a2a_send, a2a_recv, mid_send, mid_recv, fin_send, fin_recv, stat_send, stat_recv, coef_send, coef_recv,
    halo_send, halo_recv, later_send, later_recv, ring_send, ring_recv, sib_send, sib_recv,
):
    tm = lax.axis_index("tm")
    tile = lax.axis_index("tile")
    x, y = lax.rem(tm, 4), lax.div(tm, 4)
    z, core = lax.div(tile, 2), lax.rem(tile, 2)
    chans = pl.multiple_of(tile * 32, 32)
    sibling = z * 2 + (1 - core)
    right = lax.rem(z + 1, 8) * 2 + core
    left = lax.rem(z + 7, 8) * 2 + core

    def remote(src, dst, send, recv, to_tm, to_tile):
        return pltpu.make_async_remote_copy(
            src_ref=src, dst_ref=dst, send_sem=send, recv_sem=recv,
            device_id=(to_tm, to_tile), device_id_type=MESH,
        )

    load_w = pltpu.make_async_copy(w_hbm, w_ref, w_sem)
    loads = [
        pltpu.make_async_copy(src, dst, in_sem.at[i])
        for i, (src, dst) in enumerate((
            (lat_hbm, lat_ref), (gain_hbm, gain_ref), (shift_hbm, shift_ref), (bias_hbm, bias_ref),
        ))
    ]
    for load in loads:
        load.start()
    load_w.start()

    barrier = pltpu.get_barrier_semaphore()
    own_x = lax.div(tile, 4) == x

    def greet(to_tm, to_tile):
        pl.semaphore_signal(barrier, inc=1, device_id=(to_tm, to_tile), device_id_type=MESH)

    def greet_tm(k, c):
        greet(lax.rem(tm + k, 16), tile)
        return c

    def greet_a2a(k, c):
        from_tm, from_tile = y * 4 + lax.div(k, 4), x * 4 + lax.rem(k, 4)

        @pl.when(jnp.logical_not(jnp.logical_and(from_tm == tm, from_tile == tile)))
        def _():
            greet(from_tm, from_tile)

        return c

    def greet_tile(k, c):
        greet(tm, lax.rem(tile + k, 16))
        return c

    lax.fori_loop(0, 16, greet_a2a, 0)
    lax.fori_loop(1, 16, greet_tm, 0)
    lax.fori_loop(1, 16, greet_tile, 0)

    loads[0].wait()
    mine = lat_ref[...].reshape(128, 512).astype(F32)
    local_t[...] = mine.T.astype(BF)
    my_slot = x * 4 + lax.rem(tile, 4)

    def in_copy(t):
        return remote(
            local_t.at[pl.ds(pl.multiple_of(t * 32, 32), 32)], slots_in.at[my_slot],
            a2a_send, a2a_recv, y * 4 + lax.div(tile, 4), t,
        )

    def send_in(t, carry):
        to_self = jnp.logical_and(t == tile, own_x)

        @pl.when(to_self)
        def _():
            pltpu.make_async_copy(
                local_t.at[pl.ds(pl.multiple_of(t * 32, 32), 32)], slots_in.at[my_slot], a2a_recv
            ).start()

        @pl.when(jnp.logical_not(to_self))
        def _():
            in_copy(t).start()

        return carry

    pl.semaphore_wait(barrier, jnp.where(own_x, 45, 46))
    lax.fori_loop(0, 16, send_in, 0)

    for load in loads[1:]:
        load.wait()
    par_ref[...] = jnp.zeros_like(par_ref)
    par_ref[0:3, :] = gain_ref[...]
    par_ref[3:6, :] = shift_ref[...]
    columns = jnp.concatenate([par_ref[...], jnp.zeros((120, 512), F32)], axis=0)
    column_ref[...] = columns.T.reshape(8, 2, 32, 128)
    par_ref[...] = jnp.zeros_like(par_ref)
    par_ref[0:3, 0:32] = bias_ref[...]
    columns = jnp.concatenate([par_ref[:, 0:128], jnp.zeros((120, 128), F32)], axis=0)
    bias_col[...] = columns.T[0:32]

    def column(table, index):
        return jnp.sum(jnp.where(lane_of((32, 128)) == index, table, 0.0), axis=1, keepdims=True)

    def spread(owner, c):
        columns = column_ref[owner, core]
        for i in range(6):
            table_ref[i, owner] = jnp.broadcast_to(column(columns, i), (32, 128))
        return c

    lax.fori_loop(0, 8, spread, 0)

    mask_lane = lax.broadcasted_iota(jnp.int32, (128, 128), 0)
    mask_col = lax.broadcasted_iota(jnp.int32, (128, 128), 1)
    wanted = jnp.maximum(8 * y - 2 + lax.rem(mask_col, 16), 0)
    fits = (mask_lane < 16) & (mask_col < 32) & (lax.div(mask_lane, 8) == lax.div(mask_col, 16))
    for q in range(4):
        mask_ref[q] = jnp.where(fits & (8 * q + lax.rem(mask_lane, 8) <= wanted), 1.0, 0.0)

    lane128 = lane_of((32, 128))
    slot128 = lax.div(lane128, 32)

    def send_frames(part):
        for block in range(2):
            at = 512 * part + 128 * block
            one = raw[LAYERS, z, :, at:at + 128].astype(F32)
            two = raw[LAYERS, z, :, at + 256:at + 384].astype(F32)
            slots_out[part, 2 * block] = jnp.where(lane128 < 64, one, roll(two, 64)).astype(BF)
            slots_out[part, 2 * block + 1] = jnp.where(lane128 < 64, roll(one, 64), two).astype(BF)

        @pl.when(x == part)
        def _():
            mid[part] = slots_out[part]

        @pl.when(x != part)
        def _():
            remote(slots_out.at[part], mid.at[x], mid_send, mid_recv.at[x], y * 4 + part, tile).start()

    def publish(index, frames):
        sums = jnp.zeros((32, 128), F32)
        tops = [jnp.zeros((32, 128), F32)] * 2
        bots = [jnp.zeros((32, 128), F32)] * 2
        for f in range(7, -1, -1):
            values = frames(f).astype(BF)
            raw[index, z, :, 256 * f:256 * f + 256] = values
            values = values.astype(F32)
            first = jnp.sum(values, axis=1, keepdims=True)
            second = jnp.sum(values * values, axis=1, keepdims=True)
            sums = jnp.where(lane128 == f, first, sums)
            sums = jnp.where(lane128 == 8 + f, second, sums)
            slot = f // 2
            tops[f % 2] = jnp.where(slot128 == slot, roll(values[:, :128], 32 * slot), tops[f % 2])
            bots[f % 2] = jnp.where(slot128 == slot, roll(values[:, 128:], 32 * slot - 96), bots[f % 2])
        for i in range(2):
            top_out[index, :, 128 * i:128 * i + 128] = tops[i].astype(BF)
            bot_out[index, :, 128 * i:128 * i + 128] = bots[i].astype(BF)
        low = jnp.sum(sums[0:16], axis=0, keepdims=True)
        high = jnp.sum(sums[16:32], axis=0, keepdims=True)
        sub8 = lax.broadcasted_iota(jnp.int32, (8, 128), 0)
        stat_out[index] = jnp.where(sub8 == 0, low, jnp.where(sub8 == 1, high, 0.0))

    def split_w(at, c):
        layer, offset = lax.div(at, 27), lax.rem(at, 27)
        for q in range(2):
            one = w_ref[layer, offset, :, 256 * q:256 * q + 128].astype(F32)
            two = w_ref[layer, offset, :, 256 * q + 128:256 * q + 256].astype(F32)
            first = jnp.where(slot128 == 0, one, roll(one, -32))
            first = jnp.where(slot128 < 2, first, jnp.where(slot128 == 2, roll(two, 64), roll(two, 32)))
            second = jnp.where(slot128 == 0, roll(one, -32), roll(one, -64))
            second = jnp.where(slot128 < 2, second, jnp.where(slot128 == 2, roll(two, 32), two))
            wk_ref[0, layer, offset, :, 128 * q:128 * q + 128] = first.astype(BF)
            wk_ref[1, layer, offset, :, 128 * q:128 * q + 128] = second.astype(BF)
        return c

    pltpu.make_async_copy(slots_in, slots_in, a2a_recv).wait()
    halves = {}
    for part in range(4):
        for block in range(2):
            one = slots_in[part * 4 + 2 * block].astype(F32)
            two = slots_in[part * 4 + 2 * block + 1].astype(F32)
            for inner in range(2):
                if inner == 0:
                    frame = jnp.where(lane128 < 64, one, roll(two, 64))
                else:
                    frame = jnp.where(lane128 < 64, roll(one, 64), two)
                halves[2 * part + inner, block] = frame
    publish(0, lambda f: jnp.concatenate([halves[f, 0], halves[f, 1]], axis=1))

    lane256 = lane_of((32, 256))
    col256, row256 = lax.rem(lane256, 32), lax.div(lane256, 32)

    def ring_copy(layer, way, step, part):
        owner = lax.rem(z + 8 + ((1 - step) if way == 0 else (step - 1)), 8)
        piece = raw.at[layer, owner, :, slice(*PARTS[part])]
        at = (way * 4 + step - 1) * 3 + part
        return remote(
            piece, piece, ring_send.at[layer, at], ring_recv.at[layer, at], tm, right if way == 0 else left
        )

    ring_order = [
        (way, step, part)
        for step in range(1, 5) for part in range(3) for way in (0, 1)
        if step < 4 or (part == 1) == (way == 1)
    ]

    def later_copy(layer, owner):
        return remote(
            raw.at[layer, owner, :, 1536:2048], before.at[layer, owner],
            later_send.at[layer, owner], later_recv.at[layer, owner], lax.rem(y + 1, 4) * 4 + x, tile,
        )

    def sib_copy(layer, owner, kind):
        piece = y_ref.at[layer, owner, core, :, slice(*((512, LANES), (0, 512))[kind])]
        return remote(
            piece, piece, sib_send.at[layer, kind, owner], sib_recv.at[layer, kind], tm, sibling
        )

    def coef_copy(layer, k):
        to = lax.rem(z + k, 8) * 2 + core
        return remote(
            coef.at[layer, z], coef.at[layer, z], coef_send.at[layer, k], coef_recv.at[layer, k], tm, to
        )

    def halo_copies(layer):
        to_left, to_right = lax.rem(x + 3, 4), lax.rem(x + 1, 4)
        later = lax.rem(y + 1, 4)
        plan = [
            (top_out, bot_in, y * 4 + to_left), (bot_out, top_in, y * 4 + to_right),
            (top_out, bot_prev, later * 4 + to_left), (bot_out, top_prev, later * 4 + to_right),
        ]
        copies = [
            remote(src.at[layer], dst.at[layer], halo_send.at[layer, i], halo_recv.at[layer, i], to, tile)
            for i, (src, dst, to) in enumerate(plan)
        ]
        return copies

    def stat_copy(layer, k):
        other = lax.rem(tm + k, 16)
        return remote(
            stat_out.at[layer], stat_in.at[layer, 15 - k], stat_send.at[layer], stat_recv.at[layer], other, tile
        )

    low_half = lax.broadcasted_iota(jnp.int32, (32, 128), 0) < 16
    opening = y == 0

    def coefficients(layer, owner):
        table = coef[layer, owner]
        table = jnp.where(low_half, table[0:1], table[1:2])
        scaled = table * table_ref[layer, owner]
        return table, scaled, table_ref[3 + layer, owner]

    def normal_own(layer, owner):
        average, scaled, shift = coefficients(layer, owner)
        wide = jnp.concatenate([shift, shift], axis=1)
        for f in range(8):
            j = f + 2
            values = raw[layer, owner, :, 256 * f:256 * f + 256].astype(F32)
            values = (values - average[:, j:j + 1]) * scaled[:, 16 + j:17 + j] + wide
            y_ref[layer, owner, core, :, 256 * j:256 * j + 256] = silu(values).astype(BF)
        for b in range(5):
            if b == 4:
                frames = (0, 1, 0, 1)
                outside = (slot128 < 2) & (x == 0) | (slot128 >= 2) & (x == 3)
            else:
                frames = [b % 2 + 2 + 2 * s for s in range(4)]
                outside = (x == 0) if b < 2 else (x == 3)
            at = 2048 + 128 * b
            values = raw[layer, owner, :, at:at + 128].astype(F32)
            average_at, scaled_at = average[:, frames[0]:frames[0] + 1], scaled[:, 16 + frames[0]:17 + frames[0]]
            for s in range(1, 4):
                j = frames[s]
                average_at = jnp.where(slot128 == s, average[:, j:j + 1], average_at)
                scaled_at = jnp.where(slot128 == s, scaled[:, 16 + j:17 + j], scaled_at)
            values = jnp.where(outside, 0.0, silu((values - average_at) * scaled_at + shift))
            y_ref[layer, owner, core, :, MAIN + 128 * b:MAIN + 128 * b + 128] = values.astype(BF)
        sib_copy(layer, owner, 0).start()

    def normal_before(layer, owner):
        average, scaled, shift = coefficients(layer, owner)
        wide = jnp.concatenate([shift, shift], axis=1)
        for j in range(2):
            values = before[layer, owner, :, 256 * j:256 * j + 256].astype(F32)
            values = jnp.where(opening, raw[layer, owner, :, 0:256].astype(F32), values)
            values = (values - average[:, j:j + 1]) * scaled[:, 16 + j:17 + j] + wide
            y_ref[layer, owner, core, :, 256 * j:256 * j + 256] = silu(values).astype(BF)
        sib_copy(layer, owner, 1).start()

    def layer_step(layer, carry):
        halos = halo_copies(layer)
        for copy in halos:
            copy.start()
        for part in range(2):
            for way in (0, 1):
                ring_copy(layer, way, 1, part).start()

        def send_stat(k, c):
            stat_copy(layer, k).start()
            return c

        lax.fori_loop(1, 16, send_stat, 0)
        later_copy(layer, z).start()

        @pl.when(layer == 0)
        def _():
            load_w.wait()

        lax.fori_loop(27 * layer, 27 * layer + 27, split_w, 0)

        for copy in halos:
            copy.wait_recv()
        raw[layer, z, :, 2048:2304] = top_in[layer]
        raw[layer, z, :, 2304:2560] = bot_in[layer]
        values = jnp.zeros((32, 128), F32)
        for i, (now, earlier) in enumerate(((top_in, top_prev), (bot_in, bot_prev))):
            first = now[layer, :, 0:128].astype(F32)
            for b in range(2):
                last = earlier[layer, :, 128 * b:128 * b + 128].astype(F32)
                slot = 2 * i + b
                moved = jnp.where(opening, roll(first, 32 * slot), roll(last, 32 * slot - 96))
                values = jnp.where(slot128 == slot, moved, values)
        raw[layer, z, :, 2560:2688] = values.astype(BF)
        for way in (0, 1):
            ring_copy(layer, way, 1, 2).start()

        def pass_on(at_step):
            for way, step, part in ring_order:
                if step == at_step:
                    ring_copy(layer, way, step, part).wait_recv()
                    if (way, step + 1, part) in ring_order:
                        ring_copy(layer, way, step + 1, part).start()
            for way in (0, 1) if at_step < 4 else (1,):
                owner = lax.rem(z + 8 + (-at_step if way == 0 else at_step), 8)
                later_copy(layer, owner).start()

        pass_on(1)

        pltpu.make_async_copy(stat_in.at[layer], stat_in.at[layer], stat_recv.at[layer]).wait()
        sources = [jnp.zeros((8, 128), F32)] * 4
        for s in range(16):
            block = stat_out[layer] if s == 15 else stat_in[layer, s]
            from_y = lax.div(lax.rem(tm + 16 - (15 - s), 16), 4)
            for q in range(4):
                sources[q] = sources[q] + jnp.where(from_y == q, block, 0.0)
        cumulative = jnp.zeros((8, 128), F32)
        for q in range(4):
            cumulative = cumulative + lax.dot_general(
                sources[q], mask_ref[q], (((1,), (0,)), ((), ())),
                precision=lax.Precision.HIGHEST, preferred_element_type=F32,
            )
        lane8 = lane_of((8, 128))
        count = ((jnp.maximum(8 * y - 2 + lax.rem(lane8, 16), 0) + 1) * PER_FRAME).astype(F32)
        average = cumulative / count
        spread = roll(average, -16)
        inverse = lax.rsqrt(spread - average * average + EPSILON)
        coef[layer, z] = jnp.where(lane8 < 16, average, roll(inverse, 16))
        for k in (1, 7, 2, 6, 3, 5, 4):
            coef_copy(layer, k).start()
        normal_own(layer, z)
        pass_on(2)

        def both(work):
            def one(way, c):
                work(way)
                return c

            lax.fori_loop(0, 2, one, 0)

        def at_distance(step):
            return lambda way: lax.rem(z + 8 + (1 - 2 * way) * step, 8)

        def own_rows(step):
            owner = at_distance(step)
            coef_copy(layer, step).wait_recv()
            coef_copy(layer, 8 - step).wait_recv()
            both(lambda way: normal_own(layer, owner(way)))

        def rows_before(step):
            owner = at_distance(step)

            def work(way):
                later_copy(layer, owner(way)).wait_recv()
                normal_before(layer, owner(way))

            both(work)

        pass_on(3)
        own_rows(1)
        own_rows(2)
        own_rows(3)
        later_copy(layer, z).wait_recv()
        normal_before(layer, z)
        rows_before(1)
        rows_before(2)
        pass_on(4)
        far = lax.rem(z + 4, 8)
        coef_copy(layer, 4).wait_recv()
        normal_own(layer, far)

        def from_sibling(kind):
            piece = y_ref.at[layer, :, 1 - core, :, slice(*((512, LANES), (0, 512))[kind])]
            pltpu.make_async_copy(piece, piece, sib_recv.at[layer, kind]).wait()

        def product(half, first_offset, count, steps, lanes_at, width):
            total = []
            for dt in steps:
                matrix = wk_ref[half, layer, pl.ds(9 * dt + first_offset, count)].reshape(32 * count, 256)
                cells = y_ref[layer, :, half, :, lanes_at(dt)].reshape(256, width)
                total.append(lax.dot_general(
                    matrix, cells, (((1,), (0,)), ((), ())), preferred_element_type=F32
                ))
            return total

        def frame_product(half, f):
            one, two, three = product(
                half, 0, 9, range(3), lambda dt: slice(256 * (f + dt), 256 * (f + dt) + 256), 256
            )
            return one + two + three

        def edge_products(half, base, first_offset):
            return product(half, first_offset, 3, range(3), lambda dt: slice(base, base + 256), 256) + product(
                half, first_offset, 3, range(2), lambda dt: slice(PREV, PREV + 128), 128
            )

        def across(total):
            before = jnp.where(col256 >= 1, roll(total[0:32], 1), 0.0)
            after = jnp.where(col256 <= 30, roll(total[64:96], -1), 0.0)
            return before + total[32:64] + after

        def edge_rows(base, first_offset, slot):
            early, late, now, before, middle = [
                mine + theirs for mine, theirs in zip(
                    mine_edges[base], edge_products(1 - core, base, first_offset), strict=True
                )
            ]
            slots = lax.div(lane_of((96, 128)), 32)
            even = roll(early[:, :128] + late[:, 128:], 32)
            odd = roll(early[:, 128:], 32)
            even = jnp.where(slots == 0, roll(before, -32 * slot) + roll(middle, -32 * slot - 32), even)
            odd = jnp.where(slots == 0, roll(before, -32 * slot - 32), odd)
            even = even + now[:, :128]
            odd = odd + late[:, :128] + now[:, 128:]
            return across(jnp.concatenate([even, odd], axis=1))

        for f in range(7, 1, -1):
            part_ref[f] = frame_product(core, f)
        mine_edges = {base: edge_products(core, base, at) for base, at in ((TOP, 0), (BOT, 6))}
        rows_before(3)
        later_copy(layer, far).wait_recv()
        normal_before(layer, far)
        for f in (1, 0):
            part_ref[f] = frame_product(core, f)
        from_sibling(0)
        upper = edge_rows(TOP, 0, 0)
        lower = edge_rows(BOT, 6, 2)
        bias = column(bias_col[...], layer)
        keep = jnp.where(layer == 1, 1.0, 0.0)

        def frame(f):
            if f == 1:
                from_sibling(1)
            total = part_ref[f] + frame_product(1 - core, f)
            above = roll(across(total[0:96]), 32)
            below = roll(across(total[192:288]), -32)
            slot = f // 2
            edge = 128 * (f % 2)
            from_upper = roll(upper[:, edge:edge + 128], -32 * slot)
            from_lower = roll(lower[:, edge:edge + 128], 96 - 32 * slot)
            zero = jnp.zeros((32, 128), F32)
            above = jnp.where(row256 == 0, jnp.concatenate([from_upper, zero], axis=1), above)
            below = jnp.where(row256 == 7, jnp.concatenate([zero, from_lower], axis=1), below)
            result = above + across(total[96:192]) + below + bias
            return result + keep * raw[0, z, :, 256 * f:256 * f + 256].astype(F32)

        publish(layer + 1, frame)
        return carry

    lax.fori_loop(0, LAYERS, layer_step, 0)

    for part in range(4):
        send_frames(part)

    def send_rows(k, c):
        part = lax.rem(x + k, 4)

        @pl.when(k > 0)
        def _():
            pltpu.make_async_copy(mid.at[part], mid.at[part], mid_recv.at[part]).wait()

        rows = final_t.at[pl.ds(chans, 32)]
        for i in range(4):
            to_tile = part * 4 + i

            @pl.when(to_tile == tile)
            def _():
                pltpu.make_async_copy(mid.at[part, i], rows, fin_recv).start()

            @pl.when(to_tile != tile)
            def _():
                remote(mid.at[part, i], rows, fin_send, fin_recv, tm, to_tile).start()

        return c

    lax.fori_loop(0, 4, send_rows, 0)
    pltpu.make_async_copy(final_t, final_t, fin_recv).wait()
    out_ref[...] = final_t[...].astype(F32).T.astype(BF).reshape(2, 2, 32, 512)


    @pl.when(own_x)
    def _():
        pltpu.make_async_copy(slots_in.at[0:15], slots_in.at[0:15], a2a_send).wait()

    @pl.when(jnp.logical_not(own_x))
    def _():
        pltpu.make_async_copy(slots_in, slots_in, a2a_send).wait()

    pltpu.make_async_copy(slots_in.at[0:15], slots_in.at[0:15], fin_send).wait()
    pltpu.make_async_copy(mid.at[0:3], mid.at[0:3], mid_send).wait()

    def drain(layer, c):
        for copy in halo_copies(layer):
            copy.wait_send()
        pltpu.make_async_copy(stat_in.at[layer], stat_in.at[layer], stat_send.at[layer]).wait()
        for k in range(1, 8):
            coef_copy(layer, k).wait_send()
        for entry in ring_order:
            ring_copy(layer, *entry).wait_send()

        def drain_owner(owner, carry):
            later_copy(layer, owner).wait_send()
            for kind in range(2):
                sib_copy(layer, owner, kind).wait_send()
            return carry

        lax.fori_loop(0, 8, drain_owner, 0)
        return c

    lax.fori_loop(0, LAYERS, drain, 0)


def on_device(latents, norm_gain, norm_shift, conv_weight, conv_bias):
    vmem = pl.BlockSpec(memory_space=pltpu.VMEM)
    dma = pltpu.SemaphoreType.DMA
    return pl.pallas_call(
        kernel,
        out_shape=jax.ShapeDtypeStruct((2, 2, 32, 512), BF),
        in_specs=[pl.BlockSpec(memory_space=pltpu.HBM)] * 5,
        out_specs=vmem,
        scratch_shapes=[
            pltpu.VMEM((2, 2, 32, 512), BF),
            pltpu.VMEM((3, 512), F32),
            pltpu.VMEM((3, 512), F32),
            pltpu.VMEM((3, 32), F32),
            pltpu.VMEM((3, 27, 32, 512), BF),
            pltpu.VMEM((512, 128), BF),
            pltpu.VMEM((16, 32, 128), BF),
            pltpu.VMEM((4, 8, 32, SENT), BF),
            pltpu.VMEM((3, 8, 32, 512), BF),
            pltpu.VMEM((4, 32, 256), BF),
            pltpu.VMEM((4, 32, 256), BF),
            pltpu.VMEM((3, 32, 256), BF),
            pltpu.VMEM((3, 32, 256), BF),
            pltpu.VMEM((3, 32, 256), BF),
            pltpu.VMEM((3, 32, 256), BF),
            pltpu.VMEM((4, 8, 128), F32),
            pltpu.VMEM((3, 15, 8, 128), F32),
            pltpu.VMEM((4, 128, 128), F32),
            pltpu.VMEM((3, 8, 8, 128), F32),
            pltpu.VMEM((3, 8, 2, 32, LANES), BF),
            pltpu.VMEM((4, 4, 32, 128), BF),
            pltpu.VMEM((4, 4, 32, 128), BF),
            pltpu.VMEM((512, 128), BF),
            pltpu.VMEM((8, 512), F32),
            pltpu.VMEM((8, 2, 32, 128), F32),
            pltpu.VMEM((32, 128), F32),
            pltpu.VMEM((6, 8, 32, 128), F32),
            pltpu.VMEM((2, 3, 27, 32, 256), BF),
            pltpu.VMEM((8, 288, 256), F32),
            dma((4,)), dma, dma, dma, dma, dma((4,)), dma, dma, dma((3,)), dma((3,)), dma((3, 8)), dma((3, 8)),
            dma((3, 4)), dma((3, 4)), dma((3, 8)), dma((3, 8)),
            dma((3, 24)), dma((3, 24)), dma((3, 2, 8)), dma((3, 2)),
        ],
        compiler_params=pltpu.CompilerParams(
            collective_id=0, has_side_effects=True, vmem_limit_bytes=64 * 1024 * 1024
        ),
        cost_estimate=pl.CostEstimate(flops=8 * 10**9, bytes_accessed=3 * 10**6, transcendentals=10**6),
    )(latents, norm_gain, norm_shift, conv_weight, conv_bias)


def solution(mesh):
    placed = (P("tm", "tile", None, None), P(), P(), P(None, None, "tile", None), P(None, "tile"))
    return jax.shard_map(
        on_device,
        mesh=mesh,
        in_specs=placed,
        out_specs=P("tm", "tile", None, None),
        check_vma=False,
    )
```

```python
import jax
import jax.numpy as jnp
from jax import lax
from jax.experimental import pallas as pl
from jax.experimental.pallas import tpu as pltpu
from jax.sharding import PartitionSpec as P

MESH = pl.DeviceIdType.MESH
BF, F32 = jnp.bfloat16, jnp.float32
EPSILON = 1e-06
LAYERS = 3
MAIN = 10 * 256
TOP = MAIN
BOT = MAIN + 256
PREV = MAIN + 512
LANES = MAIN + 640
PARTS = ((0, 512), (512, 1024), (1024, 1536), (1536, 2048))
NPARTS = len(PARTS)
KINDS = ((512, MAIN), (0, 512), (MAIN, LANES))
PER_FRAME = 32 * 32 * 16


def lane_of(shape):
    return lax.broadcasted_iota(jnp.int32, shape, len(shape) - 1)


def roll(x, shift):
    size = x.shape[-1]
    shift = shift % size
    return x if shift == 0 else pltpu.roll(x, shift, axis=x.ndim - 1)


def silu(v):
    half = 0.5 * v
    return half + half * jnp.tanh(half)


def kernel(
    lat_hbm, gain_hbm, shift_hbm, w_hbm, bias_hbm, out_ref,
    lat_ref, gain_ref, shift_ref, bias_ref,
    w_ref, local_t, slots_in, raw, before, top_out, bot_out, top_in, bot_in, last_out, left_prev, right_prev,
    stat_out, stat_in, mask_ref, coef, y_ref, slots_out, mid, final_t, par_ref, column_ref, bias_col, table_ref, wk_ref, part_ref,
    in_sem, w_sem, a2a_send, a2a_recv, mid_send, mid_recv, fin_send, fin_recv, stat_send, stat_recv, coef_send, coef_recv,
    halo_send, halo_recv, later_send, later_recv, ring_send, ring_recv, sib_send, sib_recv,
):
    tm = lax.axis_index("tm")
    tile = lax.axis_index("tile")
    x, y = lax.rem(tm, 4), lax.div(tm, 4)
    z, core = lax.div(tile, 2), lax.rem(tile, 2)
    chans = pl.multiple_of(tile * 32, 32)
    sibling = z * 2 + (1 - core)
    right = lax.rem(z + 1, 8) * 2 + core
    left = lax.rem(z + 7, 8) * 2 + core

    def remote(src, dst, send, recv, to_tm, to_tile):
        return pltpu.make_async_remote_copy(
            src_ref=src, dst_ref=dst, send_sem=send, recv_sem=recv,
            device_id=(to_tm, to_tile), device_id_type=MESH,
        )

    load_w = pltpu.make_async_copy(w_hbm, w_ref, w_sem)
    loads = [
        pltpu.make_async_copy(src, dst, in_sem.at[i])
        for i, (src, dst) in enumerate((
            (lat_hbm, lat_ref), (gain_hbm, gain_ref), (shift_hbm, shift_ref), (bias_hbm, bias_ref),
        ))
    ]
    for load in loads:
        load.start()
    load_w.start()

    barrier = pltpu.get_barrier_semaphore()
    own_x = lax.div(tile, 4) == x

    def greet(to_tm, to_tile):
        pl.semaphore_signal(barrier, inc=1, device_id=(to_tm, to_tile), device_id_type=MESH)

    def greet_tm(k, c):
        greet(lax.rem(tm + k, 16), tile)
        return c

    def greet_a2a(k, c):
        from_tm, from_tile = y * 4 + lax.div(k, 4), x * 4 + lax.rem(k, 4)

        @pl.when(jnp.logical_not(jnp.logical_and(from_tm == tm, from_tile == tile)))
        def _():
            greet(from_tm, from_tile)

        return c

    def greet_tile(k, c):
        greet(tm, lax.rem(tile + k, 16))
        return c

    lax.fori_loop(0, 16, greet_a2a, 0)
    lax.fori_loop(1, 16, greet_tm, 0)
    lax.fori_loop(1, 16, greet_tile, 0)

    loads[0].wait()
    mine = lat_ref[...].reshape(128, 512).astype(F32)
    local_t[...] = mine.T.astype(BF)
    my_slot = x * 4 + lax.rem(tile, 4)

    def in_copy(t):
        return remote(
            local_t.at[pl.ds(pl.multiple_of(t * 32, 32), 32)], slots_in.at[my_slot],
            a2a_send, a2a_recv, y * 4 + lax.div(tile, 4), t,
        )

    def send_in(t, carry):
        to_self = jnp.logical_and(t == tile, own_x)

        @pl.when(to_self)
        def _():
            pltpu.make_async_copy(
                local_t.at[pl.ds(pl.multiple_of(t * 32, 32), 32)], slots_in.at[my_slot], a2a_recv
            ).start()

        @pl.when(jnp.logical_not(to_self))
        def _():
            in_copy(t).start()

        return carry

    pl.semaphore_wait(barrier, jnp.where(own_x, 45, 46))
    lax.fori_loop(0, 16, send_in, 0)

    for load in loads[1:]:
        load.wait()
    par_ref[...] = jnp.zeros_like(par_ref)
    par_ref[0:3, :] = gain_ref[...]
    par_ref[3:6, :] = shift_ref[...]
    columns = jnp.concatenate([par_ref[...], jnp.zeros((120, 512), F32)], axis=0)
    column_ref[...] = columns.T.reshape(8, 2, 32, 128)
    par_ref[...] = jnp.zeros_like(par_ref)
    par_ref[0:3, 0:32] = bias_ref[...]
    columns = jnp.concatenate([par_ref[:, 0:128], jnp.zeros((120, 128), F32)], axis=0)
    bias_col[...] = columns.T[0:32]

    def column(table, index):
        return jnp.sum(jnp.where(lane_of((32, 128)) == index, table, 0.0), axis=1, keepdims=True)

    def spread(owner, c):
        columns = column_ref[owner, core]
        for i in range(6):
            table_ref[i, owner] = jnp.broadcast_to(column(columns, i), (32, 128))
        return c

    lax.fori_loop(0, 8, spread, 0)

    mask_lane = lax.broadcasted_iota(jnp.int32, (128, 128), 0)
    mask_col = lax.broadcasted_iota(jnp.int32, (128, 128), 1)
    wanted = jnp.maximum(8 * y - 2 + lax.rem(mask_col, 16), 0)
    fits = (mask_lane < 16) & (mask_col < 32) & (lax.div(mask_lane, 8) == lax.div(mask_col, 16))
    for q in range(4):
        mask_ref[q] = jnp.where(fits & (8 * q + lax.rem(mask_lane, 8) <= wanted), 1.0, 0.0)

    lane128 = lane_of((32, 128))
    slot128 = lax.div(lane128, 32)

    def send_frames(part):
        for block in range(2):
            at = 512 * part + 128 * block
            one = raw[LAYERS, z, :, at:at + 128].astype(F32)
            two = raw[LAYERS, z, :, at + 256:at + 384].astype(F32)
            slots_out[part, 2 * block] = jnp.where(lane128 < 64, one, roll(two, 64)).astype(BF)
            slots_out[part, 2 * block + 1] = jnp.where(lane128 < 64, roll(one, 64), two).astype(BF)

        @pl.when(x == part)
        def _():
            mid[part] = slots_out[part]

        @pl.when(x != part)
        def _():
            remote(slots_out.at[part], mid.at[x], mid_send, mid_recv.at[x], y * 4 + part, tile).start()

    def publish(index, frames):
        sums = jnp.zeros((32, 128), F32)
        for f in range(7, -1, -1):
            values = frames(f).astype(BF)
            raw[index, z, :, 256 * f:256 * f + 256] = values
            values = values.astype(F32)
            first = jnp.sum(values, axis=1, keepdims=True)
            second = jnp.sum(values * values, axis=1, keepdims=True)
            sums = jnp.where(lane128 == f, first, sums)
            sums = jnp.where(lane128 == 8 + f, second, sums)
        low = jnp.sum(sums[0:16], axis=0, keepdims=True)
        high = jnp.sum(sums[16:32], axis=0, keepdims=True)
        sub8 = lax.broadcasted_iota(jnp.int32, (8, 128), 0)
        stat_out[index] = jnp.where(sub8 == 0, low, jnp.where(sub8 == 1, high, 0.0))

    def split_w(at, c):
        layer, offset = lax.div(at, 27), lax.rem(at, 27)
        for q in range(2):
            one = w_ref[layer, offset, :, 256 * q:256 * q + 128].astype(F32)
            two = w_ref[layer, offset, :, 256 * q + 128:256 * q + 256].astype(F32)
            first = jnp.where(slot128 == 0, one, roll(one, -32))
            first = jnp.where(slot128 < 2, first, jnp.where(slot128 == 2, roll(two, 64), roll(two, 32)))
            second = jnp.where(slot128 == 0, roll(one, -32), roll(one, -64))
            second = jnp.where(slot128 < 2, second, jnp.where(slot128 == 2, roll(two, 32), two))
            wk_ref[0, layer, offset, :, 128 * q:128 * q + 128] = first.astype(BF)
            wk_ref[1, layer, offset, :, 128 * q:128 * q + 128] = second.astype(BF)
        return c

    pltpu.make_async_copy(slots_in, slots_in, a2a_recv).wait()
    halves = {}
    for part in range(4):
        for block in range(2):
            one = slots_in[part * 4 + 2 * block].astype(F32)
            two = slots_in[part * 4 + 2 * block + 1].astype(F32)
            for inner in range(2):
                if inner == 0:
                    frame = jnp.where(lane128 < 64, one, roll(two, 64))
                else:
                    frame = jnp.where(lane128 < 64, roll(one, 64), two)
                halves[2 * part + inner, block] = frame
    publish(0, lambda f: jnp.concatenate([halves[f, 0], halves[f, 1]], axis=1))

    lane256 = lane_of((32, 256))
    col256, row256 = lax.rem(lane256, 32), lax.div(lane256, 32)

    def ring_copy(layer, way, step, part):
        owner = lax.rem(z + 8 + ((1 - step) if way == 0 else (step - 1)), 8)
        piece = raw.at[layer, owner, :, slice(*PARTS[part])]
        at = (way * 4 + step - 1) * NPARTS + part
        return remote(
            piece, piece, ring_send.at[layer, at], ring_recv.at[layer, at], tm, right if way == 0 else left
        )

    ring_order = [
        (way, step, part)
        for step in range(1, 5) for part in range(NPARTS) for way in (0, 1)
        if step < 4 or (2 * part >= NPARTS) == (way == 1)
    ]

    def later_copy(layer, owner):
        return remote(
            raw.at[layer, owner, :, 1536:2048], before.at[layer, owner],
            later_send.at[layer, owner], later_recv.at[layer, owner], lax.rem(y + 1, 4) * 4 + x, tile,
        )

    def sib_copy(layer, owner, kind):
        piece = y_ref.at[layer, owner, core, :, slice(*KINDS[kind])]
        return remote(
            piece, piece, sib_send.at[layer, kind, owner], sib_recv.at[layer, kind], tm, sibling
        )

    def coef_copy(layer, k):
        to = lax.rem(z + k, 8) * 2 + core
        return remote(
            coef.at[layer, z], coef.at[layer, z], coef_send.at[layer, k], coef_recv.at[layer, k], tm, to
        )

    def halo_copies(layer, owner):
        to_left, to_right = lax.rem(x + 3, 4), lax.rem(x + 1, 4)
        later = lax.rem(y + 1, 4)
        plan = [
            (top_out, bot_in, y * 4 + to_left), (bot_out, top_in, y * 4 + to_right),
            (last_out, right_prev, later * 4 + to_left), (last_out, left_prev, later * 4 + to_right),
        ]
        return [
            remote(
                src.at[layer, owner], dst.at[layer, owner], halo_send.at[layer, i, owner],
                halo_recv.at[layer, i, owner], to, tile,
            )
            for i, (src, dst, to) in enumerate(plan)
        ] + [later_copy(layer, owner)]

    def stat_copy(layer, k):
        other = lax.rem(tm + k, 16)
        return remote(
            stat_out.at[layer], stat_in.at[layer, 15 - k], stat_send.at[layer], stat_recv.at[layer], other, tile
        )

    low_half = lax.broadcasted_iota(jnp.int32, (32, 128), 0) < 16
    opening = y == 0

    def coefficients(layer, owner):
        table = coef[layer, owner]
        table = jnp.where(low_half, table[0:1], table[1:2])
        scaled = table * table_ref[layer, owner]
        return table, scaled, table_ref[3 + layer, owner]

    def normal_own(layer, owner):
        average, scaled, shift = coefficients(layer, owner)
        wide = jnp.concatenate([shift, shift], axis=1)
        for f in range(8):
            j = f + 2
            values = raw[layer, owner, :, 256 * f:256 * f + 256].astype(F32)
            values = (values - average[:, j:j + 1]) * scaled[:, 16 + j:17 + j] + wide
            y_ref[layer, owner, core, :, 256 * j:256 * j + 256] = silu(values).astype(BF)
        sib_copy(layer, owner, 0).start()

    def edges_out(layer, owner):
        tops = [jnp.zeros((32, 128), F32)] * 2
        bots = [jnp.zeros((32, 128), F32)] * 2
        last = jnp.zeros((32, 128), F32)
        for f in range(8):
            upper = raw[layer, owner, :, 256 * f:256 * f + 128].astype(F32)
            lower = raw[layer, owner, :, 256 * f + 128:256 * f + 256].astype(F32)
            slot = f // 2
            tops[f % 2] = jnp.where(slot128 == slot, roll(upper, 32 * slot), tops[f % 2])
            bots[f % 2] = jnp.where(slot128 == slot, roll(lower, 32 * slot - 96), bots[f % 2])
            if f >= 6:
                last = jnp.where(slot128 == f - 6, roll(upper, 32 * (f - 6)), last)
                last = jnp.where(slot128 == f - 4, roll(lower, 32 * (f - 4) - 96), last)
        for i in range(2):
            top_out[layer, owner, :, 128 * i:128 * i + 128] = tops[i].astype(BF)
            bot_out[layer, owner, :, 128 * i:128 * i + 128] = bots[i].astype(BF)
        last_out[layer, owner] = last.astype(BF)
        for copy in halo_copies(layer, owner):
            copy.start()

    def normal_late(layer, owner):
        for copy in halo_copies(layer, owner):
            copy.wait_recv()
        average, scaled, shift = coefficients(layer, owner)
        wide = jnp.concatenate([shift, shift], axis=1)
        for j in range(2):
            values = before[layer, owner, :, 256 * j:256 * j + 256].astype(F32)
            values = jnp.where(opening, raw[layer, owner, :, 0:256].astype(F32), values)
            values = (values - average[:, j:j + 1]) * scaled[:, 16 + j:17 + j] + wide
            y_ref[layer, owner, core, :, 256 * j:256 * j + 256] = silu(values).astype(BF)
        sib_copy(layer, owner, 1).start()
        for b in range(5):
            if b == 4:
                frames = (0, 1, 0, 1)
                outside = (slot128 < 2) & (x == 0) | (slot128 >= 2) & (x == 3)
                first = top_in[layer, owner, :, 0:128].astype(F32)
                second = bot_in[layer, owner, :, 0:128].astype(F32)
                starts = jnp.where(slot128 == 0, first, roll(first, 32))
                starts = jnp.where(slot128 < 2, starts, jnp.where(slot128 == 2, roll(second, 64), roll(second, 96)))
                values = jnp.where(
                    slot128 < 2, roll(left_prev[layer, owner].astype(F32), 64),
                    roll(right_prev[layer, owner].astype(F32), 64),
                )
                values = jnp.where(opening, starts, values)
            else:
                frames = [b % 2 + 2 + 2 * s for s in range(4)]
                outside = (x == 0) if b < 2 else (x == 3)
                rows = top_in if b < 2 else bot_in
                values = rows[layer, owner, :, 128 * (b % 2):128 * (b % 2) + 128].astype(F32)
            average_at, scaled_at = average[:, frames[0]:frames[0] + 1], scaled[:, 16 + frames[0]:17 + frames[0]]
            for s in range(1, 4):
                j = frames[s]
                average_at = jnp.where(slot128 == s, average[:, j:j + 1], average_at)
                scaled_at = jnp.where(slot128 == s, scaled[:, 16 + j:17 + j], scaled_at)
            values = jnp.where(outside, 0.0, silu((values - average_at) * scaled_at + shift))
            y_ref[layer, owner, core, :, MAIN + 128 * b:MAIN + 128 * b + 128] = values.astype(BF)
        sib_copy(layer, owner, 2).start()

    def layer_step(layer, carry):
        for part in range(NPARTS):
            for way in (0, 1):
                ring_copy(layer, way, 1, part).start()

        def send_stat(k, c):
            stat_copy(layer, k).start()
            return c

        lax.fori_loop(1, 16, send_stat, 0)
        edges_out(layer, z)

        @pl.when(layer == 0)
        def _():
            load_w.wait()

        lax.fori_loop(27 * layer, 27 * layer + 27, split_w, 0)

        def both(work):
            def one(way, c):
                work(way)
                return c

            lax.fori_loop(0, 2, one, 0)

        def at_distance(step):
            return lambda way: lax.rem(z + 8 + (1 - 2 * way) * step, 8)

        def pass_on(at_step):
            for way, step, part in ring_order:
                if step == at_step:
                    ring_copy(layer, way, step, part).wait_recv()
                    if (way, step + 1, part) in ring_order:
                        ring_copy(layer, way, step + 1, part).start()
            owner = at_distance(at_step)
            if at_step < 4:
                both(lambda way: edges_out(layer, owner(way)))
            else:
                edges_out(layer, owner(0))

        pass_on(1)

        pltpu.make_async_copy(stat_in.at[layer], stat_in.at[layer], stat_recv.at[layer]).wait()
        sources = [jnp.zeros((8, 128), F32)] * 4
        for s in range(16):
            block = stat_out[layer] if s == 15 else stat_in[layer, s]
            from_y = lax.div(lax.rem(tm + 16 - (15 - s), 16), 4)
            for q in range(4):
                sources[q] = sources[q] + jnp.where(from_y == q, block, 0.0)
        cumulative = jnp.zeros((8, 128), F32)
        for q in range(4):
            cumulative = cumulative + lax.dot_general(
                sources[q], mask_ref[q], (((1,), (0,)), ((), ())),
                precision=lax.Precision.HIGHEST, preferred_element_type=F32,
            )
        lane8 = lane_of((8, 128))
        count = ((jnp.maximum(8 * y - 2 + lax.rem(lane8, 16), 0) + 1) * PER_FRAME).astype(F32)
        average = cumulative / count
        spread = roll(average, -16)
        inverse = lax.rsqrt(spread - average * average + EPSILON)
        coef[layer, z] = jnp.where(lane8 < 16, average, roll(inverse, 16))
        for k in (1, 7, 2, 6, 3, 5, 4):
            coef_copy(layer, k).start()
        normal_own(layer, z)
        pass_on(2)

        def own_rows(step):
            owner = at_distance(step)
            coef_copy(layer, step).wait_recv()
            coef_copy(layer, 8 - step).wait_recv()
            both(lambda way: normal_own(layer, owner(way)))

        def late_rows(step):
            owner = at_distance(step)
            both(lambda way: normal_late(layer, owner(way)))

        pass_on(3)
        own_rows(1)
        own_rows(2)
        own_rows(3)
        normal_late(layer, z)
        late_rows(1)
        late_rows(2)
        pass_on(4)
        far = lax.rem(z + 4, 8)
        coef_copy(layer, 4).wait_recv()
        normal_own(layer, far)

        def from_sibling(kind):
            piece = y_ref.at[layer, :, 1 - core, :, slice(*KINDS[kind])]
            pltpu.make_async_copy(piece, piece, sib_recv.at[layer, kind]).wait()

        def product(half, first_offset, count, steps, lanes_at, width):
            total = []
            for dt in steps:
                matrix = wk_ref[half, layer, pl.ds(9 * dt + first_offset, count)].reshape(32 * count, 256)
                cells = y_ref[layer, :, half, :, lanes_at(dt)].reshape(256, width)
                total.append(lax.dot_general(
                    matrix, cells, (((1,), (0,)), ((), ())), preferred_element_type=F32
                ))
            return total

        def frame_product(half, f):
            one, two, three = product(
                half, 0, 9, range(3), lambda dt: slice(256 * (f + dt), 256 * (f + dt) + 256), 256
            )
            return one + two + three

        def edge_products(half, base, first_offset):
            return product(half, first_offset, 3, range(3), lambda dt: slice(base, base + 256), 256) + product(
                half, first_offset, 3, range(2), lambda dt: slice(PREV, PREV + 128), 128
            )

        def across(total):
            before = jnp.where(col256 >= 1, roll(total[0:32], 1), 0.0)
            after = jnp.where(col256 <= 30, roll(total[64:96], -1), 0.0)
            return before + total[32:64] + after

        def edge_rows(base, first_offset, slot):
            early, late, now, before, middle = [
                mine + theirs for mine, theirs in zip(
                    mine_edges[base], edge_products(1 - core, base, first_offset), strict=True
                )
            ]
            slots = lax.div(lane_of((96, 128)), 32)
            even = roll(early[:, :128] + late[:, 128:], 32)
            odd = roll(early[:, 128:], 32)
            even = jnp.where(slots == 0, roll(before, -32 * slot) + roll(middle, -32 * slot - 32), even)
            odd = jnp.where(slots == 0, roll(before, -32 * slot - 32), odd)
            even = even + now[:, :128]
            odd = odd + late[:, :128] + now[:, 128:]
            return across(jnp.concatenate([even, odd], axis=1))

        for f in range(7, 1, -1):
            part_ref[f] = frame_product(core, f)
        late_rows(3)
        normal_late(layer, far)
        for f in (1, 0):
            part_ref[f] = frame_product(core, f)
        mine_edges = {base: edge_products(core, base, at) for base, at in ((TOP, 0), (BOT, 6))}
        from_sibling(0)
        for f in range(7, 1, -1):
            part_ref[f] = part_ref[f] + frame_product(1 - core, f)
        from_sibling(1)
        from_sibling(2)
        upper = edge_rows(TOP, 0, 0)
        lower = edge_rows(BOT, 6, 2)
        bias = column(bias_col[...], layer)
        keep = jnp.where(layer == 1, 1.0, 0.0)

        def frame(f):
            total = part_ref[f]
            if f < 2:
                total = total + frame_product(1 - core, f)
            above = roll(across(total[0:96]), 32)
            below = roll(across(total[192:288]), -32)
            slot = f // 2
            edge = 128 * (f % 2)
            from_upper = roll(upper[:, edge:edge + 128], -32 * slot)
            from_lower = roll(lower[:, edge:edge + 128], 96 - 32 * slot)
            zero = jnp.zeros((32, 128), F32)
            above = jnp.where(row256 == 0, jnp.concatenate([from_upper, zero], axis=1), above)
            below = jnp.where(row256 == 7, jnp.concatenate([zero, from_lower], axis=1), below)
            result = above + across(total[96:192]) + below + bias
            return result + keep * raw[0, z, :, 256 * f:256 * f + 256].astype(F32)

        publish(layer + 1, frame)
        return carry

    lax.fori_loop(0, LAYERS, layer_step, 0)

    for part in range(4):
        send_frames(part)

    def send_rows(k, c):
        part = lax.rem(x + k, 4)

        @pl.when(k > 0)
        def _():
            pltpu.make_async_copy(mid.at[part], mid.at[part], mid_recv.at[part]).wait()

        rows = final_t.at[pl.ds(chans, 32)]
        for i in range(4):
            to_tile = part * 4 + i

            @pl.when(to_tile == tile)
            def _():
                pltpu.make_async_copy(mid.at[part, i], rows, fin_recv).start()

            @pl.when(to_tile != tile)
            def _():
                remote(mid.at[part, i], rows, fin_send, fin_recv, tm, to_tile).start()

        return c

    lax.fori_loop(0, 4, send_rows, 0)
    pltpu.make_async_copy(final_t, final_t, fin_recv).wait()
    out_ref[...] = final_t[...].astype(F32).T.astype(BF).reshape(2, 2, 32, 512)


    @pl.when(own_x)
    def _():
        pltpu.make_async_copy(slots_in.at[0:15], slots_in.at[0:15], a2a_send).wait()

    @pl.when(jnp.logical_not(own_x))
    def _():
        pltpu.make_async_copy(slots_in, slots_in, a2a_send).wait()

    pltpu.make_async_copy(slots_in.at[0:15], slots_in.at[0:15], fin_send).wait()
    pltpu.make_async_copy(mid.at[0:3], mid.at[0:3], mid_send).wait()

    def drain(layer, c):
        pltpu.make_async_copy(stat_in.at[layer], stat_in.at[layer], stat_send.at[layer]).wait()
        for k in range(1, 8):
            coef_copy(layer, k).wait_send()
        for entry in ring_order:
            ring_copy(layer, *entry).wait_send()

        def drain_owner(owner, carry):
            for copy in halo_copies(layer, owner):
                copy.wait_send()
            for kind in range(3):
                sib_copy(layer, owner, kind).wait_send()
            return carry

        lax.fori_loop(0, 8, drain_owner, 0)
        return c

    lax.fori_loop(0, LAYERS, drain, 0)


def on_device(latents, norm_gain, norm_shift, conv_weight, conv_bias):
    vmem = pl.BlockSpec(memory_space=pltpu.VMEM)
    dma = pltpu.SemaphoreType.DMA
    return pl.pallas_call(
        kernel,
        out_shape=jax.ShapeDtypeStruct((2, 2, 32, 512), BF),
        in_specs=[pl.BlockSpec(memory_space=pltpu.HBM)] * 5,
        out_specs=vmem,
        scratch_shapes=[
            pltpu.VMEM((2, 2, 32, 512), BF),
            pltpu.VMEM((3, 512), F32),
            pltpu.VMEM((3, 512), F32),
            pltpu.VMEM((3, 32), F32),
            pltpu.VMEM((3, 27, 32, 512), BF),
            pltpu.VMEM((512, 128), BF),
            pltpu.VMEM((16, 32, 128), BF),
            pltpu.VMEM((4, 8, 32, 2048), BF),
            pltpu.VMEM((3, 8, 32, 512), BF),
            pltpu.VMEM((3, 8, 32, 256), BF),
            pltpu.VMEM((3, 8, 32, 256), BF),
            pltpu.VMEM((3, 8, 32, 256), BF),
            pltpu.VMEM((3, 8, 32, 256), BF),
            pltpu.VMEM((3, 8, 32, 128), BF),
            pltpu.VMEM((3, 8, 32, 128), BF),
            pltpu.VMEM((3, 8, 32, 128), BF),
            pltpu.VMEM((4, 8, 128), F32),
            pltpu.VMEM((3, 15, 8, 128), F32),
            pltpu.VMEM((4, 128, 128), F32),
            pltpu.VMEM((3, 8, 8, 128), F32),
            pltpu.VMEM((3, 8, 2, 32, LANES), BF),
            pltpu.VMEM((4, 4, 32, 128), BF),
            pltpu.VMEM((4, 4, 32, 128), BF),
            pltpu.VMEM((512, 128), BF),
            pltpu.VMEM((8, 512), F32),
            pltpu.VMEM((8, 2, 32, 128), F32),
            pltpu.VMEM((32, 128), F32),
            pltpu.VMEM((6, 8, 32, 128), F32),
            pltpu.VMEM((2, 3, 27, 32, 256), BF),
            pltpu.VMEM((8, 288, 256), F32),
            dma((4,)), dma, dma, dma, dma, dma((4,)), dma, dma, dma((3,)), dma((3,)), dma((3, 8)), dma((3, 8)),
            dma((3, 4, 8)), dma((3, 4, 8)), dma((3, 8)), dma((3, 8)),
            dma((3, 8 * NPARTS)), dma((3, 8 * NPARTS)), dma((3, 3, 8)), dma((3, 3)),
        ],
        compiler_params=pltpu.CompilerParams(
            collective_id=0, has_side_effects=True, vmem_limit_bytes=64 * 1024 * 1024
        ),
        cost_estimate=pl.CostEstimate(flops=8 * 10**9, bytes_accessed=3 * 10**6, transcendentals=10**6),
    )(latents, norm_gain, norm_shift, conv_weight, conv_bias)


def solution(mesh):
    placed = (P("tm", "tile", None, None), P(), P(), P(None, None, "tile", None), P(None, "tile"))
    return jax.shard_map(
        on_device,
        mesh=mesh,
        in_specs=placed,
        out_specs=P("tm", "tile", None, None),
        check_vma=False,
    )
```

```python
import jax
import jax.numpy as jnp
from jax import lax
from jax.experimental import pallas as pl
from jax.experimental.pallas import tpu as pltpu
from jax.sharding import PartitionSpec as P

MESH = pl.DeviceIdType.MESH
BF, F32 = jnp.bfloat16, jnp.float32
EPSILON = 1e-06
LAYERS = 3
MAIN = 10 * 256
TOP = MAIN
BOT = MAIN + 256
PREV = MAIN + 512
LANES = MAIN + 640
PARTS = ((0, 512), (512, 1024), (1024, 1536), (1536, 2048))
NPARTS = len(PARTS)
KINDS = ((512, MAIN), (0, 512), (MAIN, LANES))
PER_FRAME = 32 * 32 * 16


def lane_of(shape):
    return lax.broadcasted_iota(jnp.int32, shape, len(shape) - 1)


def roll(x, shift):
    size = x.shape[-1]
    shift = shift % size
    return x if shift == 0 else pltpu.roll(x, shift, axis=x.ndim - 1)


def silu(v):
    half = 0.5 * v
    return half + half * jnp.tanh(half)


def kernel(
    lat_hbm, gain_hbm, shift_hbm, w_hbm, bias_hbm, out_ref,
    lat_ref, gain_ref, shift_ref, bias_ref,
    w_ref, local_t, slots_in, raw, before, top_out, bot_out, top_in, bot_in, last_out, left_prev, right_prev,
    stat_out, stat_in, mask_ref, coef, y_ref, slots_out, mid, final_t, par_ref, column_ref, bias_col, table_ref, wk_ref, part_ref, done_ref,
    in_sem, w_sem, a2a_send, a2a_recv, mid_send, mid_recv, fin_send, fin_recv, stat_send, stat_recv, coef_send, coef_recv,
    halo_send, halo_recv, later_send, later_recv, ring_send, ring_recv, sib_send, sib_recv,
):
    tm = lax.axis_index("tm")
    tile = lax.axis_index("tile")
    x, y = lax.rem(tm, 4), lax.div(tm, 4)
    z, core = lax.div(tile, 2), lax.rem(tile, 2)
    chans = pl.multiple_of(tile * 32, 32)
    sibling = z * 2 + (1 - core)
    right = lax.rem(z + 1, 8) * 2 + core
    left = lax.rem(z + 7, 8) * 2 + core

    def remote(src, dst, send, recv, to_tm, to_tile):
        return pltpu.make_async_remote_copy(
            src_ref=src, dst_ref=dst, send_sem=send, recv_sem=recv,
            device_id=(to_tm, to_tile), device_id_type=MESH,
        )

    load_w = pltpu.make_async_copy(w_hbm, w_ref, w_sem)
    loads = [
        pltpu.make_async_copy(src, dst, in_sem.at[i])
        for i, (src, dst) in enumerate((
            (lat_hbm, lat_ref), (gain_hbm, gain_ref), (shift_hbm, shift_ref), (bias_hbm, bias_ref),
        ))
    ]
    for load in loads:
        load.start()
    load_w.start()

    barrier = pltpu.get_barrier_semaphore()
    own_x = lax.div(tile, 4) == x

    def greet(to_tm, to_tile):
        pl.semaphore_signal(barrier, inc=1, device_id=(to_tm, to_tile), device_id_type=MESH)

    def greet_tm(k, c):
        greet(lax.rem(tm + k, 16), tile)
        return c

    def greet_a2a(k, c):
        from_tm, from_tile = y * 4 + lax.div(k, 4), x * 4 + lax.rem(k, 4)

        @pl.when(jnp.logical_not(jnp.logical_and(from_tm == tm, from_tile == tile)))
        def _():
            greet(from_tm, from_tile)

        return c

    def greet_tile(k, c):
        greet(tm, lax.rem(tile + k, 16))
        return c

    lax.fori_loop(0, 16, greet_a2a, 0)
    lax.fori_loop(1, 16, greet_tm, 0)
    lax.fori_loop(1, 16, greet_tile, 0)

    loads[0].wait()
    mine = lat_ref[...].reshape(128, 512).astype(F32)
    local_t[...] = mine.T.astype(BF)
    my_slot = x * 4 + lax.rem(tile, 4)

    def in_copy(t):
        return remote(
            local_t.at[pl.ds(pl.multiple_of(t * 32, 32), 32)], slots_in.at[my_slot],
            a2a_send, a2a_recv, y * 4 + lax.div(tile, 4), t,
        )

    def send_in(t, carry):
        to_self = jnp.logical_and(t == tile, own_x)

        @pl.when(to_self)
        def _():
            pltpu.make_async_copy(
                local_t.at[pl.ds(pl.multiple_of(t * 32, 32), 32)], slots_in.at[my_slot], a2a_recv
            ).start()

        @pl.when(jnp.logical_not(to_self))
        def _():
            in_copy(t).start()

        return carry

    pl.semaphore_wait(barrier, jnp.where(own_x, 45, 46))
    lax.fori_loop(0, 16, send_in, 0)

    for load in loads[1:]:
        load.wait()
    par_ref[...] = jnp.zeros_like(par_ref)
    par_ref[0:3, :] = gain_ref[...]
    par_ref[3:6, :] = shift_ref[...]
    columns = jnp.concatenate([par_ref[...], jnp.zeros((120, 512), F32)], axis=0)
    column_ref[...] = columns.T.reshape(8, 2, 32, 128)
    par_ref[...] = jnp.zeros_like(par_ref)
    par_ref[0:3, 0:32] = bias_ref[...]
    columns = jnp.concatenate([par_ref[:, 0:128], jnp.zeros((120, 128), F32)], axis=0)
    bias_col[...] = columns.T[0:32]

    def column(table, index):
        return jnp.sum(jnp.where(lane_of((32, 128)) == index, table, 0.0), axis=1, keepdims=True)

    def spread(owner, c):
        columns = column_ref[owner, core]
        for i in range(6):
            table_ref[i, owner] = jnp.broadcast_to(column(columns, i), (32, 128))
        return c

    lax.fori_loop(0, 8, spread, 0)

    mask_lane = lax.broadcasted_iota(jnp.int32, (128, 128), 0)
    mask_col = lax.broadcasted_iota(jnp.int32, (128, 128), 1)
    wanted = jnp.maximum(8 * y - 2 + lax.rem(mask_col, 16), 0)
    fits = (mask_lane < 16) & (mask_col < 32) & (lax.div(mask_lane, 8) == lax.div(mask_col, 16))
    for q in range(4):
        mask_ref[q] = jnp.where(fits & (8 * q + lax.rem(mask_lane, 8) <= wanted), 1.0, 0.0)

    lane128 = lane_of((32, 128))
    slot128 = lax.div(lane128, 32)

    def send_frames(part):
        for block in range(2):
            at = 512 * part + 128 * block
            one = raw[LAYERS, z, :, at:at + 128].astype(F32)
            two = raw[LAYERS, z, :, at + 256:at + 384].astype(F32)
            slots_out[part, 2 * block] = jnp.where(lane128 < 64, one, roll(two, 64)).astype(BF)
            slots_out[part, 2 * block + 1] = jnp.where(lane128 < 64, roll(one, 64), two).astype(BF)

        @pl.when(x == part)
        def _():
            mid[part] = slots_out[part]

        @pl.when(x != part)
        def _():
            remote(slots_out.at[part], mid.at[x], mid_send, mid_recv.at[x], y * 4 + part, tile).start()

    def publish(index, frames):
        sums = jnp.zeros((32, 128), F32)
        for f in range(7, -1, -1):
            values = frames(f).astype(BF)
            raw[index, z, :, 256 * f:256 * f + 256] = values
            values = values.astype(F32)
            first = jnp.sum(values, axis=1, keepdims=True)
            second = jnp.sum(values * values, axis=1, keepdims=True)
            sums = jnp.where(lane128 == f, first, sums)
            sums = jnp.where(lane128 == 8 + f, second, sums)
        low = jnp.sum(sums[0:16], axis=0, keepdims=True)
        high = jnp.sum(sums[16:32], axis=0, keepdims=True)
        sub8 = lax.broadcasted_iota(jnp.int32, (8, 128), 0)
        stat_out[index] = jnp.where(sub8 == 0, low, jnp.where(sub8 == 1, high, 0.0))

    def split_w(at, c):
        layer, offset = lax.div(at, 27), lax.rem(at, 27)
        for q in range(2):
            one = w_ref[layer, offset, :, 256 * q:256 * q + 128].astype(F32)
            two = w_ref[layer, offset, :, 256 * q + 128:256 * q + 256].astype(F32)
            first = jnp.where(slot128 == 0, one, roll(one, -32))
            first = jnp.where(slot128 < 2, first, jnp.where(slot128 == 2, roll(two, 64), roll(two, 32)))
            second = jnp.where(slot128 == 0, roll(one, -32), roll(one, -64))
            second = jnp.where(slot128 < 2, second, jnp.where(slot128 == 2, roll(two, 32), two))
            wk_ref[0, layer, offset, :, 128 * q:128 * q + 128] = first.astype(BF)
            wk_ref[1, layer, offset, :, 128 * q:128 * q + 128] = second.astype(BF)
        return c

    pltpu.make_async_copy(slots_in, slots_in, a2a_recv).wait()
    halves = {}
    for part in range(4):
        for block in range(2):
            one = slots_in[part * 4 + 2 * block].astype(F32)
            two = slots_in[part * 4 + 2 * block + 1].astype(F32)
            for inner in range(2):
                if inner == 0:
                    frame = jnp.where(lane128 < 64, one, roll(two, 64))
                else:
                    frame = jnp.where(lane128 < 64, roll(one, 64), two)
                halves[2 * part + inner, block] = frame
    publish(0, lambda f: jnp.concatenate([halves[f, 0], halves[f, 1]], axis=1))

    lane256 = lane_of((32, 256))
    col256, row256 = lax.rem(lane256, 32), lax.div(lane256, 32)

    def ring_copy(layer, way, step, part):
        owner = lax.rem(z + 8 + ((1 - step) if way == 0 else (step - 1)), 8)
        piece = raw.at[layer, owner, :, slice(*PARTS[part])]
        at = (way * 4 + step - 1) * NPARTS + part
        return remote(
            piece, piece, ring_send.at[layer, at], ring_recv.at[layer, at], tm, right if way == 0 else left
        )

    ring_order = [
        (way, step, part)
        for step in range(1, 5) for part in range(NPARTS) for way in (0, 1)
        if step < 4 or (2 * part >= NPARTS) == (way == 1)
    ]

    def later_copy(layer, owner):
        return remote(
            raw.at[layer, owner, :, 1536:2048], before.at[layer, owner],
            later_send.at[layer, owner], later_recv.at[layer, owner], lax.rem(y + 1, 4) * 4 + x, tile,
        )

    def sib_copy(layer, owner, kind):
        piece = y_ref.at[layer, owner, core, :, slice(*KINDS[kind])]
        return remote(
            piece, piece, sib_send.at[layer, kind, owner], sib_recv.at[layer, kind], tm, sibling
        )

    def coef_copy(layer, k):
        to = lax.rem(z + k, 8) * 2 + core
        return remote(
            coef.at[layer, z], coef.at[layer, z], coef_send.at[layer, k], coef_recv.at[layer, k], tm, to
        )

    def halo_copies(layer, owner):
        to_left, to_right = lax.rem(x + 3, 4), lax.rem(x + 1, 4)
        later = lax.rem(y + 1, 4)
        plan = [
            (top_out, bot_in, y * 4 + to_left), (bot_out, top_in, y * 4 + to_right),
            (last_out, right_prev, later * 4 + to_left), (last_out, left_prev, later * 4 + to_right),
        ]
        return [
            remote(
                src.at[layer, owner], dst.at[layer, owner], halo_send.at[layer, i, owner],
                halo_recv.at[layer, i, owner], to, tile,
            )
            for i, (src, dst, to) in enumerate(plan)
        ] + [later_copy(layer, owner)]

    def stat_copy(layer, k):
        other = lax.rem(tm + k, 16)
        return remote(
            stat_out.at[layer], stat_in.at[layer, 15 - k], stat_send.at[layer], stat_recv.at[layer], other, tile
        )

    low_half = lax.broadcasted_iota(jnp.int32, (32, 128), 0) < 16
    opening = y == 0

    def coefficients(layer, owner):
        table = coef[layer, owner]
        table = jnp.where(low_half, table[0:1], table[1:2])
        scaled = table * table_ref[layer, owner]
        return table, scaled, table_ref[3 + layer, owner]

    def normal_own(layer, owner):
        average, scaled, shift = coefficients(layer, owner)
        wide = jnp.concatenate([shift, shift], axis=1)
        for f in range(8):
            j = f + 2
            values = raw[layer, owner, :, 256 * f:256 * f + 256].astype(F32)
            values = (values - average[:, j:j + 1]) * scaled[:, 16 + j:17 + j] + wide
            y_ref[layer, owner, core, :, 256 * j:256 * j + 256] = silu(values).astype(BF)
        sib_copy(layer, owner, 0).start()

    def edges_out(layer, owner):
        tops = [jnp.zeros((32, 128), F32)] * 2
        bots = [jnp.zeros((32, 128), F32)] * 2
        last = jnp.zeros((32, 128), F32)
        for f in range(8):
            upper = raw[layer, owner, :, 256 * f:256 * f + 128].astype(F32)
            lower = raw[layer, owner, :, 256 * f + 128:256 * f + 256].astype(F32)
            slot = f // 2
            tops[f % 2] = jnp.where(slot128 == slot, roll(upper, 32 * slot), tops[f % 2])
            bots[f % 2] = jnp.where(slot128 == slot, roll(lower, 32 * slot - 96), bots[f % 2])
            if f >= 6:
                last = jnp.where(slot128 == f - 6, roll(upper, 32 * (f - 6)), last)
                last = jnp.where(slot128 == f - 4, roll(lower, 32 * (f - 4) - 96), last)
        for i in range(2):
            top_out[layer, owner, :, 128 * i:128 * i + 128] = tops[i].astype(BF)
            bot_out[layer, owner, :, 128 * i:128 * i + 128] = bots[i].astype(BF)
        last_out[layer, owner] = last.astype(BF)
        for copy in halo_copies(layer, owner):
            copy.start()

    def normal_late(layer, owner):
        for copy in halo_copies(layer, owner):
            copy.wait_recv()
        average, scaled, shift = coefficients(layer, owner)
        wide = jnp.concatenate([shift, shift], axis=1)
        for j in range(2):
            values = before[layer, owner, :, 256 * j:256 * j + 256].astype(F32)
            values = jnp.where(opening, raw[layer, owner, :, 0:256].astype(F32), values)
            values = (values - average[:, j:j + 1]) * scaled[:, 16 + j:17 + j] + wide
            y_ref[layer, owner, core, :, 256 * j:256 * j + 256] = silu(values).astype(BF)
        sib_copy(layer, owner, 1).start()
        for b in range(5):
            if b == 4:
                frames = (0, 1, 0, 1)
                outside = (slot128 < 2) & (x == 0) | (slot128 >= 2) & (x == 3)
                first = top_in[layer, owner, :, 0:128].astype(F32)
                second = bot_in[layer, owner, :, 0:128].astype(F32)
                starts = jnp.where(slot128 == 0, first, roll(first, 32))
                starts = jnp.where(slot128 < 2, starts, jnp.where(slot128 == 2, roll(second, 64), roll(second, 96)))
                values = jnp.where(
                    slot128 < 2, roll(left_prev[layer, owner].astype(F32), 64),
                    roll(right_prev[layer, owner].astype(F32), 64),
                )
                values = jnp.where(opening, starts, values)
            else:
                frames = [b % 2 + 2 + 2 * s for s in range(4)]
                outside = (x == 0) if b < 2 else (x == 3)
                rows = top_in if b < 2 else bot_in
                values = rows[layer, owner, :, 128 * (b % 2):128 * (b % 2) + 128].astype(F32)
            average_at, scaled_at = average[:, frames[0]:frames[0] + 1], scaled[:, 16 + frames[0]:17 + frames[0]]
            for s in range(1, 4):
                j = frames[s]
                average_at = jnp.where(slot128 == s, average[:, j:j + 1], average_at)
                scaled_at = jnp.where(slot128 == s, scaled[:, 16 + j:17 + j], scaled_at)
            values = jnp.where(outside, 0.0, silu((values - average_at) * scaled_at + shift))
            y_ref[layer, owner, core, :, MAIN + 128 * b:MAIN + 128 * b + 128] = values.astype(BF)
        sib_copy(layer, owner, 2).start()

    def layer_step(layer, carry):
        for part in range(NPARTS):
            for way in (0, 1):
                ring_copy(layer, way, 1, part).start()

        def send_stat(k, c):
            stat_copy(layer, k).start()
            return c

        lax.fori_loop(1, 16, send_stat, 0)
        edges_out(layer, z)

        @pl.when(layer == 0)
        def _():
            load_w.wait()

        lax.fori_loop(27 * layer, 27 * layer + 27, split_w, 0)

        def both(work):
            def one(way, c):
                work(way)
                return c

            lax.fori_loop(0, 2, one, 0)

        def at_distance(step):
            return lambda way: lax.rem(z + 8 + (1 - 2 * way) * step, 8)

        def pass_on(at_step):
            for way, step, part in ring_order:
                if step == at_step:
                    ring_copy(layer, way, step, part).wait_recv()
                    if (way, step + 1, part) in ring_order:
                        ring_copy(layer, way, step + 1, part).start()
            owner = at_distance(at_step)
            if at_step < 4:
                both(lambda way: edges_out(layer, owner(way)))
            else:
                edges_out(layer, owner(0))

        pass_on(1)

        pass_on(2)

        pltpu.make_async_copy(stat_in.at[layer], stat_in.at[layer], stat_recv.at[layer]).wait()
        sources = [jnp.zeros((8, 128), F32)] * 4
        for s in range(16):
            block = stat_out[layer] if s == 15 else stat_in[layer, s]
            from_y = lax.div(lax.rem(tm + 16 - (15 - s), 16), 4)
            for q in range(4):
                sources[q] = sources[q] + jnp.where(from_y == q, block, 0.0)
        cumulative = jnp.zeros((8, 128), F32)
        for q in range(4):
            cumulative = cumulative + lax.dot_general(
                sources[q], mask_ref[q], (((1,), (0,)), ((), ())),
                precision=lax.Precision.HIGHEST, preferred_element_type=F32,
            )
        lane8 = lane_of((8, 128))
        count = ((jnp.maximum(8 * y - 2 + lax.rem(lane8, 16), 0) + 1) * PER_FRAME).astype(F32)
        average = cumulative / count
        spread = roll(average, -16)
        inverse = lax.rsqrt(spread - average * average + EPSILON)
        coef[layer, z] = jnp.where(lane8 < 16, average, roll(inverse, 16))
        for k in (1, 7, 2, 6, 3, 5, 4):
            coef_copy(layer, k).start()
        normal_own(layer, z)

        def own_rows(step):
            owner = at_distance(step)
            coef_copy(layer, step).wait_recv()
            coef_copy(layer, 8 - step).wait_recv()
            both(lambda way: normal_own(layer, owner(way)))

        def late_rows(step):
            owner = at_distance(step)
            both(lambda way: normal_late(layer, owner(way)))

        pass_on(3)
        own_rows(1)
        own_rows(2)
        own_rows(3)
        normal_late(layer, z)
        late_rows(1)
        late_rows(2)
        pass_on(4)
        far = lax.rem(z + 4, 8)
        coef_copy(layer, 4).wait_recv()
        normal_own(layer, far)

        def from_sibling(kind):
            piece = y_ref.at[layer, :, 1 - core, :, slice(*KINDS[kind])]
            pltpu.make_async_copy(piece, piece, sib_recv.at[layer, kind]).wait()

        def product(half, first_offset, count, steps, lanes_at, width):
            total = []
            for dt in steps:
                matrix = wk_ref[half, layer, pl.ds(9 * dt + first_offset, count)].reshape(32 * count, 256)
                cells = y_ref[layer, :, half, :, lanes_at(dt)].reshape(256, width)
                total.append(lax.dot_general(
                    matrix, cells, (((1,), (0,)), ((), ())), preferred_element_type=F32
                ))
            return total

        def frame_product(half, f):
            one, two, three = product(
                half, 0, 9, range(3), lambda dt: slice(256 * (f + dt), 256 * (f + dt) + 256), 256
            )
            return one + two + three

        def edge_products(half, base, first_offset):
            return product(half, first_offset, 3, range(3), lambda dt: slice(base, base + 256), 256) + product(
                half, first_offset, 3, range(2), lambda dt: slice(PREV, PREV + 128), 128
            )

        def across(total):
            lanes = [slice(at, at + 128) for at in range(0, total.shape[1], 128)]
            before = jnp.concatenate([roll(total[0:32, at], 1) for at in lanes], axis=1)
            after = jnp.concatenate([roll(total[64:96, at], -1) for at in lanes], axis=1)
            before = jnp.where(col256 >= 1, before, 0.0)
            after = jnp.where(col256 <= 30, after, 0.0)
            return before + total[32:64] + after

        def edge_rows(base, first_offset, slot):
            early, late, now, before, middle = [
                mine + theirs for mine, theirs in zip(
                    mine_edges[base], edge_products(1 - core, base, first_offset), strict=True
                )
            ]
            slots = lax.div(lane_of((96, 128)), 32)
            even = roll(early[:, :128] + late[:, 128:], 32)
            odd = roll(early[:, 128:], 32)
            even = jnp.where(slots == 0, roll(before, -32 * slot) + roll(middle, -32 * slot - 32), even)
            odd = jnp.where(slots == 0, roll(before, -32 * slot - 32), odd)
            even = even + now[:, :128]
            odd = odd + late[:, :128] + now[:, 128:]
            return across(jnp.concatenate([even, odd], axis=1))

        def combine(total):
            above = jnp.where(row256 == 0, 0.0, roll(across(total[0:96]), 32))
            below = jnp.where(row256 == 7, 0.0, roll(across(total[192:288]), -32))
            return above + across(total[96:192]) + below

        for f in range(7, 1, -1):
            part_ref[f] = frame_product(core, f)
        late_rows(3)
        normal_late(layer, far)
        for f in (1, 0):
            part_ref[f] = frame_product(core, f)
        mine_edges = {base: edge_products(core, base, at) for base, at in ((TOP, 0), (BOT, 6))}
        from_sibling(0)
        for f in range(7, 1, -1):
            done_ref[f] = combine(part_ref[f] + frame_product(1 - core, f))
        from_sibling(1)
        from_sibling(2)
        upper = edge_rows(TOP, 0, 0)
        lower = edge_rows(BOT, 6, 2)
        bias = column(bias_col[...], layer)
        keep = jnp.where(layer == 1, 1.0, 0.0)

        def frame(f):
            body = done_ref[f] if f >= 2 else combine(part_ref[f] + frame_product(1 - core, f))
            slot = f // 2
            edge = 128 * (f % 2)
            from_upper = roll(upper[:, edge:edge + 128], -32 * slot)
            from_lower = roll(lower[:, edge:edge + 128], 96 - 32 * slot)
            edges = jnp.concatenate(
                [jnp.where(slot128 == 0, from_upper, 0.0), jnp.where(slot128 == 3, from_lower, 0.0)], axis=1
            )
            result = body + edges + bias
            return result + keep * raw[0, z, :, 256 * f:256 * f + 256].astype(F32)

        publish(layer + 1, frame)
        return carry

    lax.fori_loop(0, LAYERS, layer_step, 0)

    for part in range(4):
        send_frames(part)

    def send_rows(k, c):
        part = lax.rem(x + k, 4)

        @pl.when(k > 0)
        def _():
            pltpu.make_async_copy(mid.at[part], mid.at[part], mid_recv.at[part]).wait()

        rows = final_t.at[pl.ds(chans, 32)]
        for i in range(4):
            to_tile = part * 4 + i

            @pl.when(to_tile == tile)
            def _():
                pltpu.make_async_copy(mid.at[part, i], rows, fin_recv).start()

            @pl.when(to_tile != tile)
            def _():
                remote(mid.at[part, i], rows, fin_send, fin_recv, tm, to_tile).start()

        return c

    lax.fori_loop(0, 4, send_rows, 0)
    pltpu.make_async_copy(final_t, final_t, fin_recv).wait()
    out_ref[...] = final_t[...].astype(F32).T.astype(BF).reshape(2, 2, 32, 512)


    @pl.when(own_x)
    def _():
        pltpu.make_async_copy(slots_in.at[0:15], slots_in.at[0:15], a2a_send).wait()

    @pl.when(jnp.logical_not(own_x))
    def _():
        pltpu.make_async_copy(slots_in, slots_in, a2a_send).wait()

    pltpu.make_async_copy(slots_in.at[0:15], slots_in.at[0:15], fin_send).wait()
    pltpu.make_async_copy(mid.at[0:3], mid.at[0:3], mid_send).wait()

    def drain(layer, c):
        pltpu.make_async_copy(stat_in.at[layer], stat_in.at[layer], stat_send.at[layer]).wait()
        for k in range(1, 8):
            coef_copy(layer, k).wait_send()
        for entry in ring_order:
            ring_copy(layer, *entry).wait_send()

        def drain_owner(owner, carry):
            for copy in halo_copies(layer, owner):
                copy.wait_send()
            for kind in range(3):
                sib_copy(layer, owner, kind).wait_send()
            return carry

        lax.fori_loop(0, 8, drain_owner, 0)
        return c

    lax.fori_loop(0, LAYERS, drain, 0)


def on_device(latents, norm_gain, norm_shift, conv_weight, conv_bias):
    vmem = pl.BlockSpec(memory_space=pltpu.VMEM)
    dma = pltpu.SemaphoreType.DMA
    return pl.pallas_call(
        kernel,
        out_shape=jax.ShapeDtypeStruct((2, 2, 32, 512), BF),
        in_specs=[pl.BlockSpec(memory_space=pltpu.HBM)] * 5,
        out_specs=vmem,
        scratch_shapes=[
            pltpu.VMEM((2, 2, 32, 512), BF),
            pltpu.VMEM((3, 512), F32),
            pltpu.VMEM((3, 512), F32),
            pltpu.VMEM((3, 32), F32),
            pltpu.VMEM((3, 27, 32, 512), BF),
            pltpu.VMEM((512, 128), BF),
            pltpu.VMEM((16, 32, 128), BF),
            pltpu.VMEM((4, 8, 32, 2048), BF),
            pltpu.VMEM((3, 8, 32, 512), BF),
            pltpu.VMEM((3, 8, 32, 256), BF),
            pltpu.VMEM((3, 8, 32, 256), BF),
            pltpu.VMEM((3, 8, 32, 256), BF),
            pltpu.VMEM((3, 8, 32, 256), BF),
            pltpu.VMEM((3, 8, 32, 128), BF),
            pltpu.VMEM((3, 8, 32, 128), BF),
            pltpu.VMEM((3, 8, 32, 128), BF),
            pltpu.VMEM((4, 8, 128), F32),
            pltpu.VMEM((3, 15, 8, 128), F32),
            pltpu.VMEM((4, 128, 128), F32),
            pltpu.VMEM((3, 8, 8, 128), F32),
            pltpu.VMEM((3, 8, 2, 32, LANES), BF),
            pltpu.VMEM((4, 4, 32, 128), BF),
            pltpu.VMEM((4, 4, 32, 128), BF),
            pltpu.VMEM((512, 128), BF),
            pltpu.VMEM((8, 512), F32),
            pltpu.VMEM((8, 2, 32, 128), F32),
            pltpu.VMEM((32, 128), F32),
            pltpu.VMEM((6, 8, 32, 128), F32),
            pltpu.VMEM((2, 3, 27, 32, 256), BF),
            pltpu.VMEM((8, 288, 256), F32),
            pltpu.VMEM((8, 32, 256), F32),
            dma((4,)), dma, dma, dma, dma, dma((4,)), dma, dma, dma((3,)), dma((3,)), dma((3, 8)), dma((3, 8)),
            dma((3, 4, 8)), dma((3, 4, 8)), dma((3, 8)), dma((3, 8)),
            dma((3, 8 * NPARTS)), dma((3, 8 * NPARTS)), dma((3, 3, 8)), dma((3, 3)),
        ],
        compiler_params=pltpu.CompilerParams(
            collective_id=0, has_side_effects=True, vmem_limit_bytes=64 * 1024 * 1024
        ),
        cost_estimate=pl.CostEstimate(flops=8 * 10**9, bytes_accessed=3 * 10**6, transcendentals=10**6),
    )(latents, norm_gain, norm_shift, conv_weight, conv_bias)


def solution(mesh):
    placed = (P("tm", "tile", None, None), P(), P(), P(None, None, "tile", None), P(None, "tile"))
    return jax.shard_map(
        on_device,
        mesh=mesh,
        in_specs=placed,
        out_specs=P("tm", "tile", None, None),
        check_vma=False,
    )
```

```python
import jax
import jax.numpy as jnp
from jax import lax
from jax.experimental import pallas as pl
from jax.experimental.pallas import tpu as pltpu
from jax.sharding import PartitionSpec as P

MESH = pl.DeviceIdType.MESH
BF, F32 = jnp.bfloat16, jnp.float32
EPSILON = 1e-06
LAYERS = 3
MAIN = 10 * 256
TOP = MAIN
BOT = MAIN + 256
PREV = MAIN + 512
LANES = MAIN + 640
PARTS = ((0, 512), (512, 1024), (1024, 1536), (1536, 2048))
NPARTS = len(PARTS)
KINDS = ((512, MAIN), (0, 512), (MAIN, LANES))
PER_FRAME = 32 * 32 * 16


def lane_of(shape):
    return lax.broadcasted_iota(jnp.int32, shape, len(shape) - 1)


def roll(x, shift):
    size = x.shape[-1]
    shift = shift % size
    return x if shift == 0 else pltpu.roll(x, shift, axis=x.ndim - 1)


def silu(v):
    half = 0.5 * v
    return half + half * jnp.tanh(half)


def kernel(
    lat_hbm, gain_hbm, shift_hbm, w_hbm, bias_hbm, out_ref,
    lat_ref, gain_ref, shift_ref, bias_ref,
    w_ref, local_t, slots_in, raw, before, top_out, bot_out, top_in, bot_in, last_out, left_prev, right_prev,
    stat_out, stat_in, mask_ref, coef, y_ref, slots_out, mid, final_t, par_ref, column_ref, bias_col, table_ref, wk_ref, part_ref, done_ref,
    in_sem, w_sem, a2a_send, a2a_recv, mid_send, mid_recv, fin_send, fin_recv, stat_send, stat_recv, coef_send, coef_recv,
    halo_send, halo_recv, later_send, later_recv, ring_send, ring_recv, sib_send, sib_recv,
):
    tm = lax.axis_index("tm")
    tile = lax.axis_index("tile")
    x, y = lax.rem(tm, 4), lax.div(tm, 4)
    z, core = lax.div(tile, 2), lax.rem(tile, 2)
    chans = pl.multiple_of(tile * 32, 32)
    sibling = z * 2 + (1 - core)
    right = lax.rem(z + 1, 8) * 2 + core
    left = lax.rem(z + 7, 8) * 2 + core

    def remote(src, dst, send, recv, to_tm, to_tile):
        return pltpu.make_async_remote_copy(
            src_ref=src, dst_ref=dst, send_sem=send, recv_sem=recv,
            device_id=(to_tm, to_tile), device_id_type=MESH,
        )

    load_w = pltpu.make_async_copy(w_hbm, w_ref, w_sem)
    loads = [
        pltpu.make_async_copy(src, dst, in_sem.at[i])
        for i, (src, dst) in enumerate((
            (lat_hbm, lat_ref), (gain_hbm, gain_ref), (shift_hbm, shift_ref), (bias_hbm, bias_ref),
        ))
    ]
    for load in loads:
        load.start()
    load_w.start()

    barrier = pltpu.get_barrier_semaphore()
    own_x = lax.div(tile, 4) == x

    def greet(to_tm, to_tile):
        pl.semaphore_signal(barrier, inc=1, device_id=(to_tm, to_tile), device_id_type=MESH)

    def greet_tm(k, c):
        greet(lax.rem(tm + k, 16), tile)
        return c

    def greet_a2a(k, c):
        from_tm, from_tile = y * 4 + lax.div(k, 4), x * 4 + lax.rem(k, 4)

        @pl.when(jnp.logical_not(jnp.logical_and(from_tm == tm, from_tile == tile)))
        def _():
            greet(from_tm, from_tile)

        return c

    def greet_tile(k, c):
        greet(tm, lax.rem(tile + k, 16))
        return c

    lax.fori_loop(0, 16, greet_a2a, 0)
    lax.fori_loop(1, 16, greet_tm, 0)
    lax.fori_loop(1, 16, greet_tile, 0)

    loads[0].wait()
    mine = lat_ref[...].reshape(128, 512).astype(F32)
    local_t[...] = mine.T.astype(BF)
    my_slot = x * 4 + lax.rem(tile, 4)

    def in_copy(t):
        return remote(
            local_t.at[pl.ds(pl.multiple_of(t * 32, 32), 32)], slots_in.at[my_slot],
            a2a_send, a2a_recv, y * 4 + lax.div(tile, 4), t,
        )

    def send_in(t, carry):
        to_self = jnp.logical_and(t == tile, own_x)

        @pl.when(to_self)
        def _():
            pltpu.make_async_copy(
                local_t.at[pl.ds(pl.multiple_of(t * 32, 32), 32)], slots_in.at[my_slot], a2a_recv
            ).start()

        @pl.when(jnp.logical_not(to_self))
        def _():
            in_copy(t).start()

        return carry

    pl.semaphore_wait(barrier, jnp.where(own_x, 45, 46))
    lax.fori_loop(0, 16, send_in, 0)

    for load in loads[1:]:
        load.wait()
    par_ref[...] = jnp.zeros_like(par_ref)
    par_ref[0:3, :] = gain_ref[...]
    par_ref[3:6, :] = shift_ref[...]
    columns = jnp.concatenate([par_ref[...], jnp.zeros((120, 512), F32)], axis=0)
    column_ref[...] = columns.T.reshape(8, 2, 32, 128)
    par_ref[...] = jnp.zeros_like(par_ref)
    par_ref[0:3, 0:32] = bias_ref[...]
    columns = jnp.concatenate([par_ref[:, 0:128], jnp.zeros((120, 128), F32)], axis=0)
    bias_col[...] = columns.T[0:32]

    def column(table, index):
        return jnp.sum(jnp.where(lane_of((32, 128)) == index, table, 0.0), axis=1, keepdims=True)

    def spread(owner, c):
        columns = column_ref[owner, core]
        for i in range(6):
            table_ref[i, owner] = jnp.broadcast_to(column(columns, i), (32, 128))
        return c

    lax.fori_loop(0, 8, spread, 0)

    mask_lane = lax.broadcasted_iota(jnp.int32, (128, 128), 0)
    mask_col = lax.broadcasted_iota(jnp.int32, (128, 128), 1)
    wanted = jnp.maximum(8 * y - 2 + lax.rem(mask_col, 16), 0)
    fits = (mask_lane < 16) & (mask_col < 32) & (lax.div(mask_lane, 8) == lax.div(mask_col, 16))
    for q in range(4):
        mask_ref[q] = jnp.where(fits & (8 * q + lax.rem(mask_lane, 8) <= wanted), 1.0, 0.0)

    lane128 = lane_of((32, 128))
    slot128 = lax.div(lane128, 32)

    def send_frames(part):
        for block in range(2):
            at = 512 * part + 128 * block
            one = raw[LAYERS, z, :, at:at + 128].astype(F32)
            two = raw[LAYERS, z, :, at + 256:at + 384].astype(F32)
            slots_out[part, 2 * block] = jnp.where(lane128 < 64, one, roll(two, 64)).astype(BF)
            slots_out[part, 2 * block + 1] = jnp.where(lane128 < 64, roll(one, 64), two).astype(BF)

        @pl.when(x == part)
        def _():
            mid[part] = slots_out[part]

        @pl.when(x != part)
        def _():
            remote(slots_out.at[part], mid.at[x], mid_send, mid_recv.at[x], y * 4 + part, tile).start()

    def publish(index, frames):
        sums = jnp.zeros((32, 128), F32)
        for f in range(7, -1, -1):
            values = frames(f).astype(BF)
            raw[index, z, :, 256 * f:256 * f + 256] = values
            values = values.astype(F32)
            first = jnp.sum(values, axis=1, keepdims=True)
            second = jnp.sum(values * values, axis=1, keepdims=True)
            sums = jnp.where(lane128 == f, first, sums)
            sums = jnp.where(lane128 == 8 + f, second, sums)
        low = jnp.sum(sums[0:16], axis=0, keepdims=True)
        high = jnp.sum(sums[16:32], axis=0, keepdims=True)
        sub8 = lax.broadcasted_iota(jnp.int32, (8, 128), 0)
        stat_out[index] = jnp.where(sub8 == 0, low, jnp.where(sub8 == 1, high, 0.0))

    def split_w(at, c):
        layer, offset = lax.div(at, 27), lax.rem(at, 27)
        for q in range(2):
            one = w_ref[layer, offset, :, 256 * q:256 * q + 128].astype(F32)
            two = w_ref[layer, offset, :, 256 * q + 128:256 * q + 256].astype(F32)
            first = jnp.where(slot128 == 0, one, roll(one, -32))
            first = jnp.where(slot128 < 2, first, jnp.where(slot128 == 2, roll(two, 64), roll(two, 32)))
            second = jnp.where(slot128 == 0, roll(one, -32), roll(one, -64))
            second = jnp.where(slot128 < 2, second, jnp.where(slot128 == 2, roll(two, 32), two))
            wk_ref[0, layer, offset, :, 128 * q:128 * q + 128] = first.astype(BF)
            wk_ref[1, layer, offset, :, 128 * q:128 * q + 128] = second.astype(BF)
        return c

    pltpu.make_async_copy(slots_in, slots_in, a2a_recv).wait()
    halves = {}
    for part in range(4):
        for block in range(2):
            one = slots_in[part * 4 + 2 * block].astype(F32)
            two = slots_in[part * 4 + 2 * block + 1].astype(F32)
            for inner in range(2):
                if inner == 0:
                    frame = jnp.where(lane128 < 64, one, roll(two, 64))
                else:
                    frame = jnp.where(lane128 < 64, roll(one, 64), two)
                halves[2 * part + inner, block] = frame
    publish(0, lambda f: jnp.concatenate([halves[f, 0], halves[f, 1]], axis=1))

    lane256 = lane_of((32, 256))
    col256, row256 = lax.rem(lane256, 32), lax.div(lane256, 32)

    def ring_copy(layer, way, step, part):
        owner = lax.rem(z + 8 + ((1 - step) if way == 0 else (step - 1)), 8)
        piece = raw.at[layer, owner, :, slice(*PARTS[part])]
        at = (way * 4 + step - 1) * NPARTS + part
        return remote(
            piece, piece, ring_send.at[layer, at], ring_recv.at[layer, at], tm, right if way == 0 else left
        )

    ring_order = [
        (way, step, part)
        for step in range(1, 5) for part in range(NPARTS) for way in (0, 1)
        if step < 4 or (2 * part >= NPARTS) == (way == 1)
    ]

    def later_copy(layer, owner):
        return remote(
            raw.at[layer, owner, :, 1536:2048], before.at[layer, owner],
            later_send.at[layer, owner], later_recv.at[layer, owner], lax.rem(y + 1, 4) * 4 + x, tile,
        )

    def sib_copy(layer, owner, kind):
        piece = y_ref.at[layer, owner, core, :, slice(*KINDS[kind])]
        return remote(
            piece, piece, sib_send.at[layer, kind, owner], sib_recv.at[layer, kind], tm, sibling
        )

    def coef_copy(layer, k):
        to = lax.rem(z + k, 8) * 2 + core
        return remote(
            coef.at[layer, z], coef.at[layer, z], coef_send.at[layer, k], coef_recv.at[layer, k], tm, to
        )

    def halo_copies(layer, owner):
        to_left, to_right = lax.rem(x + 3, 4), lax.rem(x + 1, 4)
        later = lax.rem(y + 1, 4)
        plan = [
            (top_out, bot_in, y * 4 + to_left), (bot_out, top_in, y * 4 + to_right),
            (last_out, right_prev, later * 4 + to_left), (last_out, left_prev, later * 4 + to_right),
        ]
        return [
            remote(
                src.at[layer, owner], dst.at[layer, owner], halo_send.at[layer, i, owner],
                halo_recv.at[layer, i, owner], to, tile,
            )
            for i, (src, dst, to) in enumerate(plan)
        ] + [later_copy(layer, owner)]

    def stat_copy(layer, k):
        other = lax.rem(tm + k, 16)
        return remote(
            stat_out.at[layer], stat_in.at[layer, 15 - k], stat_send.at[layer], stat_recv.at[layer], other, tile
        )

    low_half = lax.broadcasted_iota(jnp.int32, (32, 128), 0) < 16
    opening = y == 0

    def coefficients(layer, owner):
        table = coef[layer, owner]
        table = jnp.where(low_half, table[0:1], table[1:2])
        scaled = table * table_ref[layer, owner]
        return table, scaled, table_ref[3 + layer, owner]

    def normal_own(layer, owner):
        average, scaled, shift = coefficients(layer, owner)
        wide = jnp.concatenate([shift, shift], axis=1)
        for f in range(8):
            j = f + 2
            values = raw[layer, owner, :, 256 * f:256 * f + 256].astype(F32)
            values = (values - average[:, j:j + 1]) * scaled[:, 16 + j:17 + j] + wide
            y_ref[layer, owner, core, :, 256 * j:256 * j + 256] = silu(values).astype(BF)
        sib_copy(layer, owner, 0).start()

    def edges_out(layer, owner):
        tops = [jnp.zeros((32, 128), F32)] * 2
        bots = [jnp.zeros((32, 128), F32)] * 2
        last = jnp.zeros((32, 128), F32)
        for f in range(8):
            upper = raw[layer, owner, :, 256 * f:256 * f + 128].astype(F32)
            lower = raw[layer, owner, :, 256 * f + 128:256 * f + 256].astype(F32)
            slot = f // 2
            tops[f % 2] = jnp.where(slot128 == slot, roll(upper, 32 * slot), tops[f % 2])
            bots[f % 2] = jnp.where(slot128 == slot, roll(lower, 32 * slot - 96), bots[f % 2])
            if f >= 6:
                last = jnp.where(slot128 == f - 6, roll(upper, 32 * (f - 6)), last)
                last = jnp.where(slot128 == f - 4, roll(lower, 32 * (f - 4) - 96), last)
        for i in range(2):
            top_out[layer, owner, :, 128 * i:128 * i + 128] = tops[i].astype(BF)
            bot_out[layer, owner, :, 128 * i:128 * i + 128] = bots[i].astype(BF)
        last_out[layer, owner] = last.astype(BF)
        for copy in halo_copies(layer, owner):
            copy.start()

    def normal_late(layer, owner):
        for copy in halo_copies(layer, owner):
            copy.wait_recv()
        average, scaled, shift = coefficients(layer, owner)
        wide = jnp.concatenate([shift, shift], axis=1)
        for j in range(2):
            values = before[layer, owner, :, 256 * j:256 * j + 256].astype(F32)
            values = jnp.where(opening, raw[layer, owner, :, 0:256].astype(F32), values)
            values = (values - average[:, j:j + 1]) * scaled[:, 16 + j:17 + j] + wide
            y_ref[layer, owner, core, :, 256 * j:256 * j + 256] = silu(values).astype(BF)
        sib_copy(layer, owner, 1).start()
        for b in range(5):
            if b == 4:
                frames = (0, 1, 0, 1)
                outside = (slot128 < 2) & (x == 0) | (slot128 >= 2) & (x == 3)
                first = top_in[layer, owner, :, 0:128].astype(F32)
                second = bot_in[layer, owner, :, 0:128].astype(F32)
                starts = jnp.where(slot128 == 0, first, roll(first, 32))
                starts = jnp.where(slot128 < 2, starts, jnp.where(slot128 == 2, roll(second, 64), roll(second, 96)))
                values = jnp.where(
                    slot128 < 2, roll(left_prev[layer, owner].astype(F32), 64),
                    roll(right_prev[layer, owner].astype(F32), 64),
                )
                values = jnp.where(opening, starts, values)
            else:
                frames = [b % 2 + 2 + 2 * s for s in range(4)]
                outside = (x == 0) if b < 2 else (x == 3)
                rows = top_in if b < 2 else bot_in
                values = rows[layer, owner, :, 128 * (b % 2):128 * (b % 2) + 128].astype(F32)
            average_at, scaled_at = average[:, frames[0]:frames[0] + 1], scaled[:, 16 + frames[0]:17 + frames[0]]
            for s in range(1, 4):
                j = frames[s]
                average_at = jnp.where(slot128 == s, average[:, j:j + 1], average_at)
                scaled_at = jnp.where(slot128 == s, scaled[:, 16 + j:17 + j], scaled_at)
            values = jnp.where(outside, 0.0, silu((values - average_at) * scaled_at + shift))
            y_ref[layer, owner, core, :, MAIN + 128 * b:MAIN + 128 * b + 128] = values.astype(BF)
        sib_copy(layer, owner, 2).start()

    def layer_step(layer, carry):
        for part in range(NPARTS):
            for way in (0, 1):
                ring_copy(layer, way, 1, part).start()

        edges_out(layer, z)

        def send_stat(k, c):
            stat_copy(layer, k).start()
            return c

        lax.fori_loop(1, 16, send_stat, 0)

        @pl.when(layer == 0)
        def _():
            load_w.wait()

        lax.fori_loop(27 * layer, 27 * layer + 27, split_w, 0)

        def both(work):
            def one(way, c):
                work(way)
                return c

            lax.fori_loop(0, 2, one, 0)

        def at_distance(step):
            return lambda way: lax.rem(z + 8 + (1 - 2 * way) * step, 8)

        def pass_on(at_step):
            for way, step, part in ring_order:
                if step == at_step:
                    ring_copy(layer, way, step, part).wait_recv()
                    if (way, step + 1, part) in ring_order:
                        ring_copy(layer, way, step + 1, part).start()
            owner = at_distance(at_step)
            if at_step < 4:
                both(lambda way: edges_out(layer, owner(way)))
            else:
                edges_out(layer, owner(0))

        pass_on(1)

        pass_on(2)

        pltpu.make_async_copy(stat_in.at[layer], stat_in.at[layer], stat_recv.at[layer]).wait()
        sources = [jnp.zeros((8, 128), F32)] * 4
        for s in range(16):
            block = stat_out[layer] if s == 15 else stat_in[layer, s]
            from_y = lax.div(lax.rem(tm + 16 - (15 - s), 16), 4)
            for q in range(4):
                sources[q] = sources[q] + jnp.where(from_y == q, block, 0.0)
        cumulative = jnp.zeros((8, 128), F32)
        for q in range(4):
            cumulative = cumulative + lax.dot_general(
                sources[q], mask_ref[q], (((1,), (0,)), ((), ())),
                precision=lax.Precision.HIGHEST, preferred_element_type=F32,
            )
        lane8 = lane_of((8, 128))
        count = ((jnp.maximum(8 * y - 2 + lax.rem(lane8, 16), 0) + 1) * PER_FRAME).astype(F32)
        average = cumulative / count
        spread = roll(average, -16)
        inverse = lax.rsqrt(spread - average * average + EPSILON)
        coef[layer, z] = jnp.where(lane8 < 16, average, roll(inverse, 16))
        for k in (1, 7, 2, 6, 3, 5, 4):
            coef_copy(layer, k).start()
        normal_own(layer, z)

        def own_rows(step):
            owner = at_distance(step)
            coef_copy(layer, step).wait_recv()
            coef_copy(layer, 8 - step).wait_recv()
            both(lambda way: normal_own(layer, owner(way)))

        def late_rows(step):
            owner = at_distance(step)
            both(lambda way: normal_late(layer, owner(way)))

        pass_on(3)
        own_rows(1)
        own_rows(2)
        own_rows(3)
        normal_late(layer, z)
        late_rows(1)
        late_rows(2)
        pass_on(4)
        far = lax.rem(z + 4, 8)
        coef_copy(layer, 4).wait_recv()
        normal_own(layer, far)

        def from_sibling(kind):
            piece = y_ref.at[layer, :, 1 - core, :, slice(*KINDS[kind])]
            pltpu.make_async_copy(piece, piece, sib_recv.at[layer, kind]).wait()

        def product(half, first_offset, count, steps, lanes_at, width):
            total = []
            for dt in steps:
                matrix = wk_ref[half, layer, pl.ds(9 * dt + first_offset, count)].reshape(32 * count, 256)
                cells = y_ref[layer, :, half, :, lanes_at(dt)].reshape(256, width)
                total.append(lax.dot_general(
                    matrix, cells, (((1,), (0,)), ((), ())), preferred_element_type=F32
                ))
            return total

        def frame_product(half, f):
            one, two, three = product(
                half, 0, 9, range(3), lambda dt: slice(256 * (f + dt), 256 * (f + dt) + 256), 256
            )
            return one + two + three

        def edge_products(half, base, first_offset):
            return product(half, first_offset, 3, range(3), lambda dt: slice(base, base + 256), 256) + product(
                half, first_offset, 3, range(2), lambda dt: slice(PREV, PREV + 128), 128
            )

        def across(total):
            lanes = [slice(at, at + 128) for at in range(0, total.shape[1], 128)]
            before = jnp.concatenate([roll(total[0:32, at], 1) for at in lanes], axis=1)
            after = jnp.concatenate([roll(total[64:96, at], -1) for at in lanes], axis=1)
            before = jnp.where(col256 >= 1, before, 0.0)
            after = jnp.where(col256 <= 30, after, 0.0)
            return before + total[32:64] + after

        def edge_rows(base, first_offset, slot):
            early, late, now, before, middle = [
                mine + theirs for mine, theirs in zip(
                    mine_edges[base], edge_products(1 - core, base, first_offset), strict=True
                )
            ]
            slots = lax.div(lane_of((96, 128)), 32)
            even = roll(early[:, :128] + late[:, 128:], 32)
            odd = roll(early[:, 128:], 32)
            even = jnp.where(slots == 0, roll(before, -32 * slot) + roll(middle, -32 * slot - 32), even)
            odd = jnp.where(slots == 0, roll(before, -32 * slot - 32), odd)
            even = even + now[:, :128]
            odd = odd + late[:, :128] + now[:, 128:]
            return across(jnp.concatenate([even, odd], axis=1))

        def combine(total):
            above = jnp.where(row256 == 0, 0.0, roll(across(total[0:96]), 32))
            below = jnp.where(row256 == 7, 0.0, roll(across(total[192:288]), -32))
            return above + across(total[96:192]) + below

        for f in range(7, 1, -1):
            part_ref[f] = frame_product(core, f)
        late_rows(3)
        normal_late(layer, far)
        for f in (1, 0):
            part_ref[f] = frame_product(core, f)
        mine_edges = {base: edge_products(core, base, at) for base, at in ((TOP, 0), (BOT, 6))}
        from_sibling(0)
        for f in range(7, 1, -1):
            done_ref[f] = combine(part_ref[f] + frame_product(1 - core, f))
        from_sibling(1)
        from_sibling(2)
        upper = edge_rows(TOP, 0, 0)
        lower = edge_rows(BOT, 6, 2)
        bias = column(bias_col[...], layer)
        keep = jnp.where(layer == 1, 1.0, 0.0)

        def frame(f):
            body = done_ref[f] if f >= 2 else combine(part_ref[f] + frame_product(1 - core, f))
            slot = f // 2
            edge = 128 * (f % 2)
            from_upper = roll(upper[:, edge:edge + 128], -32 * slot)
            from_lower = roll(lower[:, edge:edge + 128], 96 - 32 * slot)
            edges = jnp.concatenate(
                [jnp.where(slot128 == 0, from_upper, 0.0), jnp.where(slot128 == 3, from_lower, 0.0)], axis=1
            )
            result = body + edges + bias
            return result + keep * raw[0, z, :, 256 * f:256 * f + 256].astype(F32)

        publish(layer + 1, frame)
        return carry

    lax.fori_loop(0, LAYERS, layer_step, 0)

    for part in range(4):
        send_frames(part)

    def send_rows(k, c):
        part = lax.rem(x + k, 4)

        @pl.when(k > 0)
        def _():
            pltpu.make_async_copy(mid.at[part], mid.at[part], mid_recv.at[part]).wait()

        rows = final_t.at[pl.ds(chans, 32)]
        for i in range(4):
            to_tile = part * 4 + i

            @pl.when(to_tile == tile)
            def _():
                pltpu.make_async_copy(mid.at[part, i], rows, fin_recv).start()

            @pl.when(to_tile != tile)
            def _():
                remote(mid.at[part, i], rows, fin_send, fin_recv, tm, to_tile).start()

        return c

    lax.fori_loop(0, 4, send_rows, 0)
    pltpu.make_async_copy(final_t, final_t, fin_recv).wait()
    out_ref[...] = final_t[...].astype(F32).T.astype(BF).reshape(2, 2, 32, 512)


    @pl.when(own_x)
    def _():
        pltpu.make_async_copy(slots_in.at[0:15], slots_in.at[0:15], a2a_send).wait()

    @pl.when(jnp.logical_not(own_x))
    def _():
        pltpu.make_async_copy(slots_in, slots_in, a2a_send).wait()

    pltpu.make_async_copy(slots_in.at[0:15], slots_in.at[0:15], fin_send).wait()
    pltpu.make_async_copy(mid.at[0:3], mid.at[0:3], mid_send).wait()

    def drain(layer, c):
        pltpu.make_async_copy(stat_in.at[layer], stat_in.at[layer], stat_send.at[layer]).wait()
        for k in range(1, 8):
            coef_copy(layer, k).wait_send()
        for entry in ring_order:
            ring_copy(layer, *entry).wait_send()

        def drain_owner(owner, carry):
            for copy in halo_copies(layer, owner):
                copy.wait_send()
            for kind in range(3):
                sib_copy(layer, owner, kind).wait_send()
            return carry

        lax.fori_loop(0, 8, drain_owner, 0)
        return c

    lax.fori_loop(0, LAYERS, drain, 0)


def on_device(latents, norm_gain, norm_shift, conv_weight, conv_bias):
    vmem = pl.BlockSpec(memory_space=pltpu.VMEM)
    dma = pltpu.SemaphoreType.DMA
    return pl.pallas_call(
        kernel,
        out_shape=jax.ShapeDtypeStruct((2, 2, 32, 512), BF),
        in_specs=[pl.BlockSpec(memory_space=pltpu.HBM)] * 5,
        out_specs=vmem,
        scratch_shapes=[
            pltpu.VMEM((2, 2, 32, 512), BF),
            pltpu.VMEM((3, 512), F32),
            pltpu.VMEM((3, 512), F32),
            pltpu.VMEM((3, 32), F32),
            pltpu.VMEM((3, 27, 32, 512), BF),
            pltpu.VMEM((512, 128), BF),
            pltpu.VMEM((16, 32, 128), BF),
            pltpu.VMEM((4, 8, 32, 2048), BF),
            pltpu.VMEM((3, 8, 32, 512), BF),
            pltpu.VMEM((3, 8, 32, 256), BF),
            pltpu.VMEM((3, 8, 32, 256), BF),
            pltpu.VMEM((3, 8, 32, 256), BF),
            pltpu.VMEM((3, 8, 32, 256), BF),
            pltpu.VMEM((3, 8, 32, 128), BF),
            pltpu.VMEM((3, 8, 32, 128), BF),
            pltpu.VMEM((3, 8, 32, 128), BF),
            pltpu.VMEM((4, 8, 128), F32),
            pltpu.VMEM((3, 15, 8, 128), F32),
            pltpu.VMEM((4, 128, 128), F32),
            pltpu.VMEM((3, 8, 8, 128), F32),
            pltpu.VMEM((3, 8, 2, 32, LANES), BF),
            pltpu.VMEM((4, 4, 32, 128), BF),
            pltpu.VMEM((4, 4, 32, 128), BF),
            pltpu.VMEM((512, 128), BF),
            pltpu.VMEM((8, 512), F32),
            pltpu.VMEM((8, 2, 32, 128), F32),
            pltpu.VMEM((32, 128), F32),
            pltpu.VMEM((6, 8, 32, 128), F32),
            pltpu.VMEM((2, 3, 27, 32, 256), BF),
            pltpu.VMEM((8, 288, 256), F32),
            pltpu.VMEM((8, 32, 256), F32),
            dma((4,)), dma, dma, dma, dma, dma((4,)), dma, dma, dma((3,)), dma((3,)), dma((3, 8)), dma((3, 8)),
            dma((3, 4, 8)), dma((3, 4, 8)), dma((3, 8)), dma((3, 8)),
            dma((3, 8 * NPARTS)), dma((3, 8 * NPARTS)), dma((3, 3, 8)), dma((3, 3)),
        ],
        compiler_params=pltpu.CompilerParams(
            collective_id=0, has_side_effects=True, vmem_limit_bytes=64 * 1024 * 1024
        ),
        cost_estimate=pl.CostEstimate(flops=8 * 10**9, bytes_accessed=3 * 10**6, transcendentals=10**6),
    )(latents, norm_gain, norm_shift, conv_weight, conv_bias)


def solution(mesh):
    placed = (P("tm", "tile", None, None), P(), P(), P(None, None, "tile", None), P(None, "tile"))
    return jax.shard_map(
        on_device,
        mesh=mesh,
        in_specs=placed,
        out_specs=P("tm", "tile", None, None),
        check_vma=False,
    )
```
